256 devices in a mesh: tile: 32 (over x_lo, z, core), corner: 8 (over y, x_hi).
Axes of the slice: x: 4 (x_hi: 2, x_lo: 2; x = x_hi * 2 + x_lo), y: 4, z: 8, core: 2. Of those that a mesh axis runs over, the one named last changes fastest.
Arguments:
- mask_logits: float32 [4096, 1024], P('tile'), may hold values from -4 to 4
- target: int32 [4096, 1024], P('tile'), may hold values 0 or 1
- kernels: float32 [4, 12, 25, 384], replicated, may hold values from -0.9 to 0.9
- dose_levels: float32 [4], replicated, may hold values from 0.8 to 1.2
Outputs:
- pv_band: float32 [4096, 1024], P('tile', 'corner')
- logit_grad: float32 [4096, 1024], P('tile', 'corner')
The draws below stay inside these ranges and needn't reach their ends.
All inputs are finite; a program needn't handle non-finite values. No bound on the sum of `target` on one device may be relied on, other than what follows from the above.
Results may differ from the reference program's by a relative error of at most 0.024.
Values may be sent and summed in bfloat16 or wider, within the bound.
No kernel may reach another device: no remote copies, remote signals or barrier semaphores. Data moves between devices by JAX's collectives and lax.ppermute only.
A program may use at most 128 MiB of HBM per device.

```python
import math
import jax
import jax.numpy as jnp
from jax import lax

W = 1024
NF = 192
NK = 12
KS = 25
NFOC = 4
NDOSE = 4
CORNERS = 16
NROWS = 4096


def place_ends(array, stream_key, least, top_value):
    dims = array.shape
    place = [jax.random.randint(jax.random.fold_in(stream_key, axis), (), 0, dims[axis]) for axis in range(len(dims))]
    array = array.at[tuple(place)].set(least)
    longest = dims.index(max(dims))
    place[longest] = (place[longest] + 1) % dims[longest]
    return array.at[tuple(place)].set(top_value)


def block_levels(own_key, extent, shards, low, top_value):
    gain, own = 1.0, jax.random.fold_in(own_key, 6)
    for dim, parts in shards:
        heights = jnp.exp(jax.random.uniform(jax.random.fold_in(own, dim), (parts,), jnp.float32, low / len(shards), top_value / len(shards)))
        gain = gain * jnp.repeat(heights, extent[dim] // parts).reshape([-1 if axis == dim else 1 for axis in range(len(extent))])
    return gain


def gaussian(key, shape, scale, bound, cuts=(), kind=jnp.bfloat16):
    entries = jax.random.normal(key, shape, jnp.float32) * scale
    if len(cuts) > 0:
        entries = block_levels(key, shape, cuts, -0.22, 0.18) * entries
    return jnp.clip(entries, min=-bound, max=bound).astype(kind)


def setup_inputs(seed: int = 0) -> dict:
    arg_keys = jax.random.split(jax.random.key(seed), 5)
    mask_logits = gaussian(arg_keys[0], (NROWS, W), 1.0, 4.0, ((0, 32),), jnp.float32)
    target = place_ends((jax.random.randint(arg_keys[1], (NROWS, W), 0, 2) < 1).astype(jnp.int32), jax.random.fold_in(arg_keys[1], 1), 0, 1)
    kernels = gaussian(arg_keys[2], (NFOC, NK, KS, 2 * NF), 0.15, 0.9, (), jnp.float32)
    dose_levels = jnp.clip(jax.random.uniform(arg_keys[3], (NDOSE,), jnp.float32, 0.8, 1.2), 0.8, 1.2)
    return dict(mask_logits=mask_logits, target=target, kernels=kernels, dose_levels=dose_levels)


STEEPNESS = 4.0
THRESHOLD = 1.0
SHARPNESS = 12.0

def dft_tables(columns, half_freq):
    column_ids = jnp.arange(columns, dtype=jnp.int32)
    frequencies = jnp.arange(half_freq, dtype=jnp.int32) - half_freq // 2
    phases = frequencies[:, None] * column_ids[None, :] % columns
    angles = 2.0 * math.pi / columns * phases.astype(jnp.float32)
    factor = 1.0 / math.sqrt(columns)
    cosine = jnp.cos(angles) * factor
    sine_table = jnp.sin(angles) * factor
    forward = jnp.concatenate([cosine.T, -sine_table.T], axis=1)
    inverse = jnp.concatenate([jnp.concatenate([cosine, sine_table], axis=1), jnp.concatenate([-sine_table, cosine], axis=1)], axis=0)
    return (forward, inverse)

def mix_rows(extended, kernel):
    kernel_taps = kernel.shape[0]
    half_freq = kernel.shape[1] // 2
    row_count = extended.shape[0] - kernel_taps + 1
    field_re = None
    field_im = None
    for offset in range(kernel_taps):
        ext_re = extended[offset:offset + row_count, :half_freq]
        ext_im = extended[offset:offset + row_count, half_freq:]
        kern_re = kernel[offset, :half_freq]
        kern_im = kernel[offset, half_freq:]
        part_re = ext_re * kern_re - ext_im * kern_im
        part_im = ext_re * kern_im + ext_im * kern_re
        field_re = part_re if field_re is None else field_re + part_re
        field_im = part_im if field_im is None else field_im + part_im
    return jnp.concatenate([field_re, field_im], axis=1)

def unmix_rows(mixed_grad, kernel):
    kernel_taps = kernel.shape[0]
    half_freq = kernel.shape[1] // 2
    grad_re = mixed_grad[:, :half_freq]
    grad_im = mixed_grad[:, half_freq:]
    summed = None
    for offset in range(kernel_taps):
        kern_re = kernel[offset, :half_freq]
        kern_im = kernel[offset, half_freq:]
        back_re = grad_re * kern_re + grad_im * kern_im
        back_im = grad_im * kern_re - grad_re * kern_im
        padded = jnp.pad(jnp.concatenate([back_re, back_im], axis=1), ((offset, kernel_taps - 1 - offset), (0, 0)))
        summed = padded if summed is None else summed + padded
    return summed

def bf_dot(left, right):
    return jnp.dot(left.astype(jnp.float32), right.astype(jnp.float32), preferred_element_type=jnp.float32, precision=lax.Precision.HIGHEST)

def reference(mask_logits, target, kernels, dose_levels):
    columns = mask_logits.shape[1]
    half_freq = kernels.shape[3] // 2
    rim_rows = kernels.shape[2] // 2
    forward, inverse = dft_tables(columns, half_freq)
    forward_low = forward.astype(jnp.bfloat16)
    inverse_low = inverse.astype(jnp.bfloat16)
    mask_field = jnp.tanh(mask_logits)
    mask_low = mask_field.astype(jnp.bfloat16)
    spectra = bf_dot(mask_low, forward_low).astype(jnp.bfloat16)
    extended = jnp.pad(spectra.astype(jnp.float32), ((rim_rows, rim_rows), (0, 0)))

    def intensity(kernel_set):

        def advance(summed, kernel):
            mixed = mix_rows(extended, kernel).astype(jnp.bfloat16)
            fields = bf_dot(mixed, inverse_low)
            return (summed + fields[:, :columns] ** 2 + fields[:, columns:] ** 2, None)
        start_sum = jnp.zeros(mask_logits.shape, jnp.float32)
        return lax.scan(advance, start_sum, kernel_set)[0]
    levels = jnp.stack([intensity(kernels[focus]) for focus in range(NFOC)])
    resists = []
    dose_values = []
    soft_high = jnp.zeros(mask_logits.shape, jnp.float32)
    soft_low = jnp.zeros(mask_logits.shape, jnp.float32)
    for corner in range(CORNERS):
        dose_value = dose_levels[corner % NDOSE]
        aerial = levels[corner // NDOSE]
        resist = jax.nn.sigmoid(STEEPNESS * (dose_value * aerial - THRESHOLD))
        resists.append(resist)
        dose_values.append(dose_value)
        soft_high = soft_high + jnp.exp(SHARPNESS * resist)
        soft_low = soft_low + jnp.exp(-SHARPNESS * resist)
    top_band = jnp.log(soft_high) / SHARPNESS
    bottom_band = -jnp.log(soft_low) / SHARPNESS
    pv_band = top_band - bottom_band
    wanted = target.astype(jnp.float32)
    high_weight = (top_band - wanted) / soft_high
    low_weight = (bottom_band - wanted) / soft_low
    ext_grad = jnp.zeros(extended.shape, jnp.float32)
    for corner in range(CORNERS):
        resist = resists[corner]
        resist_grad = high_weight * jnp.exp(SHARPNESS * resist) + low_weight * jnp.exp(-SHARPNESS * resist)
        aerial_grad = resist_grad * STEEPNESS * dose_values[corner] * resist * (1.0 - resist)
        doubled = 2.0 * jnp.concatenate([aerial_grad, aerial_grad], axis=1)

        def advance_back(summed, kernel):
            mixed = mix_rows(extended, kernel).astype(jnp.bfloat16)
            fields = bf_dot(mixed, inverse_low)
            field_grad = (doubled * fields).astype(jnp.bfloat16)
            mixed_grad = bf_dot(field_grad, inverse_low.T)
            return (summed + unmix_rows(mixed_grad, kernel), None)
        ext_grad = lax.scan(advance_back, ext_grad, kernels[corner // NDOSE])[0]
    spectra_grad = ext_grad[rim_rows:rim_rows + mask_logits.shape[0]]
    mask_grad = jnp.dot(spectra_grad, forward.T, preferred_element_type=jnp.float32, precision=lax.Precision.HIGHEST)
    return (pv_band, mask_grad * (1.0 - mask_field ** 2))
```

```python
import math

import jax
import jax.numpy as jnp
import numpy as np
from jax import lax
from jax.experimental import pallas as pl
from jax.experimental.pallas import tpu as pltpu
from jax.sharding import PartitionSpec as P

STEEPNESS = 4.0
THRESHOLD = 1.0
SHARPNESS = 12.0

BF = jnp.bfloat16
F32 = jnp.float32

W = 1024
NF = 192
LANES = 256
TAPS = 25
RIM = TAPS // 2
ROWS = 128
NK = 12
NFOC = 4
NDOSE = 4
SHARE = 19
PAIR = 20
U = 48
GRID = 384
EDGE = 32
TEDGE = 16
MSG = 48 + 32
TURN = 1.62425


def low(table):
    return jnp.asarray(np.asarray(table, np.float32)).astype(BF)


def low_parts(table):
    table = np.asarray(table, np.float32)
    high = table.astype(jnp.bfloat16)
    return jnp.asarray(high), jnp.asarray((table - high.astype(np.float32)).astype(jnp.bfloat16))


def forward_table():
    phase = np.outer(np.arange(NF) - NF // 2, np.arange(W)) % W
    angle = 2.0 * math.pi * phase / W
    scale = 1.0 / math.sqrt(W)
    table = np.zeros((W, 2 * LANES))
    table[:, :NF] = scale * np.cos(angle).T
    table[:, LANES : LANES + NF] = -scale * np.sin(angle).T
    return table


def inverse_table():
    phase = np.outer(np.arange(NF) - NF // 2, np.arange(GRID)) % GRID
    angle = 2.0 * math.pi * phase / GRID
    scale = 1.0 / math.sqrt(W)
    table = np.zeros((2 * LANES, 2 * GRID))
    table[:NF, :GRID] = scale * np.cos(angle)
    table[:NF, GRID:] = scale * np.sin(angle)
    table[LANES : LANES + NF, :GRID] = -scale * np.sin(angle)
    table[LANES : LANES + NF, GRID:] = scale * np.cos(angle)
    return table


def interpolation_table():
    where = np.arange(W)[None, :] / W - np.arange(GRID)[:, None] / GRID
    orders = np.arange(1, NF)
    table = np.ones((GRID, W))
    for order in orders:
        table += 2.0 * np.cos(2.0 * math.pi * order * where)
    return table / GRID


def row_angles(left, right):
    return 2.0 * math.pi * (np.outer(np.arange(left), np.arange(right)) % U) / U


def tap_table(count=4):
    angle = row_angles(U, TAPS)
    table = np.zeros((count * U, count * 64))
    for q in range(count):
        table[q * U : (q + 1) * U, q * 64 : q * 64 + TAPS] = np.cos(angle)
        table[q * U : (q + 1) * U, q * 64 + 32 : q * 64 + 32 + TAPS] = np.sin(angle)
    return TURN * table


def window_table():
    angle = row_angles(U, U)
    return TURN * np.concatenate([np.cos(angle), -np.sin(angle)], axis=1)


def back_table():
    angle = row_angles(U, U)
    return TURN * np.concatenate([np.cos(angle), np.sin(angle)], axis=1)


def mix_table(count=2):
    angle = row_angles(PAIR, U)
    table = np.zeros((count * PAIR, count * 2 * U))
    for q in range(count):
        rows = slice(q * PAIR, (q + 1) * PAIR)
        table[rows, q * 2 * U : q * 2 * U + U] = np.cos(angle)
        table[rows, q * 2 * U + U : (q + 1) * 2 * U] = np.sin(angle)
    return TURN * table


def unmix_table(count=4):
    angle = row_angles(U, PAIR)
    half = count * PAIR
    table = np.zeros((count * U, 2 * half))
    for q in range(count):
        rows = slice(q * U, (q + 1) * U)
        table[rows, q * PAIR : (q + 1) * PAIR] = np.cos(angle)
        table[rows, half + q * PAIR : half + (q + 1) * PAIR] = -np.sin(angle)
    return TURN * table


def dot(left, right):
    return jnp.dot(left, right, preferred_element_type=F32)


def dot_nt(left, right):
    return lax.dot_general(left, right, (((1,), (1,)), ((), ())), preferred_element_type=F32)


def turned(value):
    value = value.astype(BF)
    swapped = jnp.concatenate([-value[:, LANES:], value[:, :LANES]], axis=1)
    return jnp.concatenate([value, swapped], axis=0)


def picked(count, length, first):
    row = lax.broadcasted_iota(jnp.int32, (count, length), 0) + first
    row = jnp.where(row >= length, row - length, row)
    column = lax.broadcasted_iota(jnp.int32, (count, length), 1)
    return jnp.where(row == column, 1.0, 0.0).astype(BF)


def edge_kernel(mask_ref, target_ref, out_ref, mask_rows, target_rows, sems):
    down = lax.axis_index("corner") < lax.axis_size("corner") // 2
    mask_from = pl.multiple_of(jnp.where(down, ROWS - EDGE, 0), EDGE)
    target_from = pl.multiple_of(jnp.where(down, ROWS - TEDGE, 0), TEDGE)
    copies = [
        pltpu.make_async_copy(mask_ref.at[pl.ds(mask_from, EDGE)], mask_rows, sems.at[0]),
        pltpu.make_async_copy(target_ref.at[pl.ds(target_from, TEDGE)], target_rows, sems.at[1]),
    ]
    for copy in copies:
        copy.start()
    for copy in copies:
        copy.wait()
    out_ref[:EDGE] = jnp.tanh(mask_rows[...]).astype(BF)
    out_ref[EDGE:] = target_rows[...].astype(F32).astype(BF)


def prepare_kernel(kernels_ref, mask_ref, forward_ref, tap_ref, hat_ref, spectra_ref, slope_ref, stack_ref):
    stack_ref[...] = jnp.zeros_like(stack_ref)
    for group in range(NFOC * NK // 4):
        slot = group % 2
        for q in range(4):
            taps = kernels_ref[group * 4 + q]
            re = taps[:, :NF]
            im = taps[:, NF:]
            base = q * 64
            stack_ref[slot, base : base + TAPS, :NF] = re
            stack_ref[slot, base : base + TAPS, LANES : LANES + NF] = im
            stack_ref[slot, base + 32 : base + 32 + TAPS, :NF] = -im
            stack_ref[slot, base + 32 : base + 32 + TAPS, LANES : LANES + NF] = re
        hat = dot(tap_ref[...], stack_ref[slot].astype(BF)).astype(BF)
        hat_ref[group * 4 : group * 4 + 4] = hat.reshape(4, U, 2 * LANES)
    field = jnp.tanh(mask_ref[...])
    spectra_ref[...] = dot(field.astype(BF), forward_ref[...]).astype(BF)
    column = pl.multiple_of(lax.axis_index("corner") * ROWS, ROWS)
    share = jnp.tanh(mask_ref[:, pl.ds(column, ROWS)])
    slope_ref[...] = 1.0 - share * share


def image_kernel(
    dose_ref,
    edge_ref,
    spectra_ref,
    target_ref,
    hat_ref,
    forward_ref,
    inverse_ref,
    interp_ref,
    interp_low_ref,
    window_ref,
    mix_ref,
    unmix_ref,
    back_ref,
    out_ref,
    mixed_ref,
    field_ref,
    aerial_ref,
    grad_ref,
    fold_ref,
    band_ref,
):
    corner = lax.axis_index("corner")
    tile = lax.axis_index("tile")
    edge = dot(edge_ref[:EDGE], forward_ref[...]).astype(BF)
    rows = jnp.concatenate([edge, spectra_ref[...]], axis=0)
    pick = picked(U, ROWS + EDGE, SHARE * corner + (EDGE - 2 * RIM))
    mask_hat = dot(window_ref[...], turned(dot(pick, rows))) * (1.0 / (TURN * TURN * TURN * U))
    mask_re = mask_hat[:, :LANES]
    mask_im = mask_hat[:, LANES:]
    for group in range(NFOC * NK // 4):
        parts = []
        for pair in range(2):
            stack = []
            for q in range(2):
                hat = hat_ref[group * 4 + pair * 2 + q].astype(F32)
                hat_re = hat[:, :LANES]
                hat_im = hat[:, LANES:]
                re = (mask_re * hat_re - mask_im * hat_im).astype(BF)
                im = (mask_re * hat_im + mask_im * hat_re).astype(BF)
                stack.append(jnp.concatenate([re, im], axis=1))
                stack.append(jnp.concatenate([-im, re], axis=1))
            parts.append(dot(mix_ref[...], jnp.concatenate(stack, axis=0)))
        mixed_ref[group * 4 * PAIR : (group + 1) * 4 * PAIR] = jnp.concatenate(parts, axis=0).astype(BF)
    per_focus = NK * PAIR
    fold_ref[...] = jnp.zeros_like(fold_ref)
    for focus in range(NFOC):
        fields = dot(mixed_ref[focus * per_focus : (focus + 1) * per_focus], inverse_ref[...])
        field_ref[focus * per_focus : (focus + 1) * per_focus] = fields
        power = fields[:, :GRID] * fields[:, :GRID] + fields[:, GRID:] * fields[:, GRID:]
        summed = power[: 2 * PAIR]
        for pair in range(1, NK // 2):
            summed = summed + power[pair * 2 * PAIR : (pair + 1) * 2 * PAIR]
        fold_ref[focus, : 2 * PAIR] = summed
        aerial_ref[focus * 24 : (focus + 1) * 24, :GRID] = (
            fold_ref[focus, 0:24] + fold_ref[focus, PAIR : PAIR + 24]
        )
    coarse = aerial_ref[:, :GRID]
    coarse_high = coarse.astype(BF)
    coarse_low = (coarse - coarse_high.astype(F32)).astype(BF)
    both = dot(jnp.concatenate([coarse_high, coarse_low], axis=0), interp_ref[...])
    aerial_ref[...] = both[: NFOC * 24] + both[NFOC * 24 :] + dot(coarse_high, interp_low_ref[...])
    wanted_rows = jnp.concatenate([edge_ref[EDGE:], target_ref[...].astype(F32).astype(BF)], axis=0)
    pick = picked(24, ROWS + TEDGE, SHARE * corner + (TEDGE - RIM))
    band_ref[...] = dot(pick, wanted_rows)
    local = lax.broadcasted_iota(jnp.int32, (24, ROWS), 0)
    pixel = tile * ROWS + SHARE * corner - RIM + local
    valid = (local < SHARE) & (pixel >= 0) & (pixel < ROWS * lax.axis_size("tile"))
    valid = jnp.where(valid, 1.0, 0.0)
    doses = [dose_ref[d] for d in range(NDOSE)]
    for chunk in range(W // ROWS):
        cols = slice(chunk * ROWS, (chunk + 1) * ROWS)
        high = None
        low_sum = None
        kept = []
        for focus in range(NFOC):
            aerial = aerial_ref[focus * 24 : (focus + 1) * 24, cols]
            for d in range(NDOSE):
                level = (0.5 * STEEPNESS * doses[d]) * aerial - 0.5 * STEEPNESS * THRESHOLD
                resist = 0.5 * jnp.tanh(level) + 0.5
                up = jnp.exp(SHARPNESS * resist)
                down = jnp.exp(-SHARPNESS * resist)
                high = up if high is None else high + up
                low_sum = down if low_sum is None else low_sum + down
                kept.append((resist, up, down))
        wanted = band_ref[:, cols]
        top = jnp.log(high) / SHARPNESS
        bottom = -jnp.log(low_sum) / SHARPNESS
        band_ref[:, cols] = top - bottom
        high_weight = valid * (top - wanted) / high
        low_weight = valid * (bottom - wanted) / low_sum
        for focus in range(NFOC):
            total = None
            for d in range(NDOSE):
                resist, up, down = kept[focus * NDOSE + d]
                term = (high_weight * up + low_weight * down) * (resist * (1.0 - resist))
                term = term * (2.0 * STEEPNESS * doses[d])
                total = term if total is None else total + term
            grad_ref[focus * 24 : (focus + 1) * 24, cols] = total
    coarse_grad = dot_nt(grad_ref[...].astype(BF), interp_ref[...])
    acc_re = jnp.zeros((U, LANES), F32)
    acc_im = jnp.zeros((U, LANES), F32)
    for focus in range(NFOC):
        part = coarse_grad[focus * 24 : (focus + 1) * 24]
        fold_ref[focus, 0:24] = part
        fold_ref[focus, PAIR : PAIR + 24] = part
        twice = fold_ref[focus, : 2 * PAIR]
        twice = jnp.concatenate([twice, twice], axis=1)
        twice = jnp.concatenate([twice, twice], axis=0)
        for group in range(NK // 4):
            start = focus * per_focus + group * 4 * PAIR
            field_grad = (twice * field_ref[start : start + 4 * PAIR]).astype(BF)
            mixed_grad = dot_nt(field_grad, inverse_ref[...])
            hats = dot(unmix_ref[...], turned(mixed_grad))
            for q in range(4):
                grad_re = hats[q * U : (q + 1) * U, :LANES]
                grad_im = hats[q * U : (q + 1) * U, LANES:]
                hat = hat_ref[focus * NK + group * 4 + q].astype(F32)
                hat_re = hat[:, :LANES]
                hat_im = hat[:, LANES:]
                acc_re = acc_re + (grad_re * hat_re + grad_im * hat_im)
                acc_im = acc_im + (grad_im * hat_re - grad_re * hat_im)
    acc = jnp.concatenate([acc_re, acc_im], axis=1) * (1.0 / (TURN * TURN * TURN * U))
    spectra_grad = dot(back_ref[...], turned(acc))
    mask_grad = dot_nt(spectra_grad.astype(BF), forward_ref[...]).astype(BF)
    for block in range(W // ROWS):
        cols = slice(block * ROWS, (block + 1) * ROWS)
        out_ref[block, :U] = mask_grad[:, cols]
        band = jnp.concatenate([band_ref[:, cols], jnp.zeros((8, ROWS), F32)], axis=0)
        out_ref[block, U:] = band.astype(BF)


def finish_kernel(blocks_ref, slope_ref, band_ref, grad_ref, sum_ref, rows_ref):
    sum_ref[...] = jnp.zeros_like(sum_ref)
    for source in range(blocks_ref.shape[0]):
        block = blocks_ref[source].astype(F32)
        start = SHARE * source
        sum_ref[start : start + U] = sum_ref[start : start + U] + block[:U]
        rows_ref[start : start + 24] = block[U : U + 24]
    grad_ref[...] = sum_ref[2 * RIM : 2 * RIM + ROWS] * slope_ref[...]
    band_ref[...] = rows_ref[RIM : RIM + ROWS]


def params(mib):
    return pltpu.CompilerParams(vmem_limit_bytes=mib << 20)


def whole(count):
    return [pl.BlockSpec(memory_space=pltpu.VMEM)] * count


def per_device(mask_logits, target, kernels, dose_levels):
    tiles = lax.axis_size("tile")
    corners = lax.axis_size("corner")
    edge = pl.pallas_call(
        edge_kernel,
        name="edge",
        out_shape=jax.ShapeDtypeStruct((EDGE + TEDGE, W), BF),
        in_specs=[pl.BlockSpec(memory_space=pl.ANY)] * 2,
        out_specs=pl.BlockSpec(memory_space=pltpu.VMEM),
        scratch_shapes=[
            pltpu.VMEM((EDGE, W), F32),
            pltpu.VMEM((TEDGE, W), jnp.int32),
            pltpu.SemaphoreType.DMA((2,)),
        ],
    )(mask_logits, target)
    pairs = []
    for i in range(tiles - 1):
        for c in range(corners):
            begin = SHARE * c - 2 * RIM
            if begin < 0:
                pairs.append((i * corners + c, (i + 1) * corners + c))
            elif begin + SHARE + 2 * RIM > ROWS:
                pairs.append(((i + 1) * corners + c, i * corners + c))
    edge = lax.ppermute(edge, ("tile", "corner"), pairs)
    forward = low(forward_table())
    inverse = low(inverse_table())
    interp, interp_low = low_parts(interpolation_table())
    count = NFOC * NK
    hats, spectra, slope = pl.pallas_call(
        prepare_kernel,
        name="prepare",
        out_shape=(
            jax.ShapeDtypeStruct((count, U, 2 * LANES), BF),
            jax.ShapeDtypeStruct((ROWS, 2 * LANES), BF),
            jax.ShapeDtypeStruct((ROWS, ROWS), F32),
        ),
        in_specs=whole(4),
        out_specs=tuple(whole(3)),
        scratch_shapes=[pltpu.VMEM((2, 256, 2 * LANES), F32)],
        compiler_params=params(24),
        cost_estimate=pl.CostEstimate(flops=2_000_000_000, bytes_accessed=8_000_000, transcendentals=0),
    )(kernels.reshape(count, TAPS, 2 * NF), mask_logits, forward, low(tap_table()))
    blocks = pl.pallas_call(
        image_kernel,
        name="image",
        out_shape=jax.ShapeDtypeStruct((W // ROWS, MSG, ROWS), BF),
        in_specs=[pl.BlockSpec(memory_space=pltpu.SMEM)] + whole(12),
        out_specs=pl.BlockSpec(memory_space=pltpu.VMEM),
        scratch_shapes=[
            pltpu.VMEM((count * PAIR, 2 * LANES), BF),
            pltpu.VMEM((count * PAIR, 2 * GRID), F32),
            pltpu.VMEM((NFOC * 24, W), F32),
            pltpu.VMEM((NFOC * 24, W), F32),
            pltpu.VMEM((NFOC, U, GRID), F32),
            pltpu.VMEM((24, W), F32),
        ],
        compiler_params=params(32),
        cost_estimate=pl.CostEstimate(flops=4_000_000_000, bytes_accessed=8_000_000, transcendentals=0),
    )(
        dose_levels,
        edge,
        spectra,
        target,
        hats,
        forward,
        inverse,
        interp,
        interp_low,
        low(window_table()),
        low(mix_table()),
        low(unmix_table()),
        low(back_table()),
    )
    blocks = lax.all_to_all(blocks, "corner", 0, 0, tiled=True)
    return pl.pallas_call(
        finish_kernel,
        name="finish",
        out_shape=(
            jax.ShapeDtypeStruct((ROWS, ROWS), F32),
            jax.ShapeDtypeStruct((ROWS, ROWS), F32),
        ),
        in_specs=whole(2),
        out_specs=tuple(whole(2)),
        scratch_shapes=[pltpu.VMEM((192, ROWS), F32), pltpu.VMEM((160, ROWS), F32)],
    )(blocks, slope)


def solution(mesh):
    return jax.shard_map(
        per_device,
        mesh=mesh,
        in_specs=(P("tile", None), P("tile", None), P(), P()),
        out_specs=(P("tile", "corner"), P("tile", "corner")),
        check_vma=False,
    )
```

```python
import math

import jax
import jax.numpy as jnp
import numpy as np
from jax import lax
from jax.experimental import pallas as pl
from jax.experimental.pallas import tpu as pltpu
from jax.sharding import PartitionSpec as P

STEEPNESS = 4.0
THRESHOLD = 1.0
SHARPNESS = 12.0

BF = jnp.bfloat16
F32 = jnp.float32

W = 1024
NF = 192
LANES = 256
TAPS = 25
RIM = TAPS // 2
ROWS = 128
NK = 12
NFOC = 4
NDOSE = 4
SHARE = 19
PAIR = 20
TAP_ROWS = 112
U = 48
GRID = 384
EDGE = 32
TEDGE = 16
MSG = 48 + 32
TURN = 1.62425


def low(table):
    return jnp.asarray(np.asarray(table, np.float32)).astype(BF)


def forward_table():
    phase = np.outer(np.arange(NF) - NF // 2, np.arange(W)) % W
    angle = 2.0 * math.pi * phase / W
    scale = 1.0 / math.sqrt(W)
    table = np.zeros((W, 2 * LANES))
    table[:, :NF] = scale * np.cos(angle).T
    table[:, LANES : LANES + NF] = -scale * np.sin(angle).T
    return table


def inverse_table():
    phase = np.outer(np.arange(NF) - NF // 2, np.arange(GRID)) % GRID
    angle = 2.0 * math.pi * phase / GRID
    scale = 1.0 / math.sqrt(W)
    table = np.zeros((2 * LANES, 2 * GRID))
    table[:NF, :GRID] = scale * np.cos(angle)
    table[:NF, GRID:] = scale * np.sin(angle)
    table[LANES : LANES + NF, :GRID] = -scale * np.sin(angle)
    table[LANES : LANES + NF, GRID:] = scale * np.cos(angle)
    return table


def interpolation_table():
    where = np.arange(W)[None, :] / W - np.arange(GRID)[:, None] / GRID
    orders = np.arange(1, NF)
    table = np.ones((GRID, W))
    for order in orders:
        table += 2.0 * np.cos(2.0 * math.pi * order * where)
    return table / GRID


def row_angles(left, right):
    return 2.0 * math.pi * (np.outer(np.arange(left), np.arange(right)) % U) / U


def tap_table():
    angle = row_angles(U, TAPS)
    table = np.zeros((NFOC, U, 2, TAP_ROWS))
    for focus in range(NFOC):
        table[focus, :, 0, focus : TAPS * NFOC : NFOC] = np.cos(angle)
        table[focus, :, 1, focus : TAPS * NFOC : NFOC] = np.sin(angle)
    return TURN * table.reshape(NFOC * U, 2 * TAP_ROWS)


def window_table():
    angle = row_angles(U, U)
    return TURN * np.concatenate([np.cos(angle), -np.sin(angle)], axis=1)


def back_table():
    angle = row_angles(U, U)
    return TURN * np.concatenate([np.cos(angle), np.sin(angle)], axis=1)


def mix_table(count=2):
    angle = row_angles(PAIR, U)
    table = np.zeros((count * PAIR, count * 2 * U))
    for q in range(count):
        rows = slice(q * PAIR, (q + 1) * PAIR)
        table[rows, q * 2 * U : q * 2 * U + U] = np.cos(angle)
        table[rows, q * 2 * U + U : (q + 1) * 2 * U] = np.sin(angle)
    return TURN * table


def unmix_table(count=4):
    angle = row_angles(U, PAIR)
    half = count * PAIR
    table = np.zeros((count * U, 2 * half))
    for q in range(count):
        rows = slice(q * U, (q + 1) * U)
        table[rows, q * PAIR : (q + 1) * PAIR] = np.cos(angle)
        table[rows, half + q * PAIR : half + (q + 1) * PAIR] = -np.sin(angle)
    return TURN * table


def placing_tables(count):
    grad = np.zeros((ROWS, count, U))
    band = np.zeros((ROWS, count, MSG - U))
    for source in range(count):
        for row in range(SHARE + 2 * RIM):
            pixel = SHARE * source + row - 2 * RIM
            if 0 <= pixel < ROWS:
                grad[pixel, source, row] = 1.0
        for row in range(SHARE):
            pixel = SHARE * source + row - RIM
            if 0 <= pixel < ROWS:
                band[pixel, source, row] = 1.0
    return grad.reshape(ROWS, -1), band.reshape(ROWS, -1)


def dot(left, right):
    return jnp.dot(left, right, preferred_element_type=F32)


def turned(value):
    value = value.astype(BF)
    swapped = jnp.concatenate([-value[:, LANES:], value[:, :LANES]], axis=1)
    return jnp.concatenate([value, swapped], axis=0)


def picked(count, length, first):
    row = lax.broadcasted_iota(jnp.int32, (count, length), 0) + first
    row = jnp.where(row >= length, row - length, row)
    column = lax.broadcasted_iota(jnp.int32, (count, length), 1)
    return jnp.where(row == column, 1.0, 0.0).astype(BF)


def edge_kernel(mask_ref, target_ref, dose_ref, out_ref, dose_rows_ref, mask_rows, target_rows, doses, sems):
    down = lax.axis_index("corner") < lax.axis_size("corner") // 2
    mask_from = pl.multiple_of(jnp.where(down, ROWS - EDGE, 0), EDGE)
    target_from = pl.multiple_of(jnp.where(down, ROWS - TEDGE, 0), TEDGE)
    copies = [
        pltpu.make_async_copy(mask_ref.at[pl.ds(mask_from, EDGE)], mask_rows, sems.at[0]),
        pltpu.make_async_copy(target_ref.at[pl.ds(target_from, TEDGE)], target_rows, sems.at[1]),
        pltpu.make_async_copy(dose_ref, doses, sems.at[2]),
    ]
    for copy in copies:
        copy.start()
    for copy in copies:
        copy.wait()
    out_ref[:EDGE] = jnp.tanh(mask_rows[...]).astype(BF)
    out_ref[EDGE:] = target_rows[...].astype(F32).astype(BF)
    for d in range(NDOSE):
        dose_rows_ref[d : d + 1] = jnp.full((1, ROWS), doses[d])


def prepare_kernel(
    kernels_ref, mask_ref, forward_ref, tap_ref, hat_ref, spectra_ref, slope_ref, taps_ref, share_ref, sem
):
    column = pl.multiple_of(lax.axis_index("corner") * ROWS, ROWS)
    share = jnp.tanh(mask_ref[:, pl.ds(column, ROWS)])
    share_ref[...] = 1.0 - share * share
    copy = pltpu.make_async_copy(share_ref, slope_ref, sem)
    copy.start()
    lane = lax.broadcasted_iota(jnp.int32, (TAP_ROWS, LANES), 1)
    taps_ref[:, NFOC * TAPS - 4 :] = jnp.zeros((2, TAP_ROWS - NFOC * TAPS + 4, 2 * NF), F32)
    for kernel in range(NK):
        slot = kernel % 2
        for tap in range(TAPS):
            taps_ref[slot, tap * NFOC : (tap + 1) * NFOC] = kernels_ref[kernel, tap]
        taps = taps_ref[slot]
        re = jnp.where(lane < NF, taps[:, :LANES], 0.0)
        im = jnp.where(lane < NF, pltpu.roll(taps, NF, 1)[:, :LANES], 0.0)
        hat = dot(tap_ref[...], turned(jnp.concatenate([re, im], axis=1))).astype(BF)
        hat_ref[kernel * NFOC : (kernel + 1) * NFOC] = hat.reshape(NFOC, U, 2 * LANES)
    field = jnp.tanh(mask_ref[...])
    spectra_ref[...] = dot(field.astype(BF), forward_ref[...]).astype(BF)
    copy.wait()


def image_kernel(
    dose_ref,
    edge_ref,
    spectra_ref,
    target_ref,
    hat_ref,
    forward_ref,
    inverse_ref,
    interp_ref,
    forward_t_ref,
    inverse_t_ref,
    interp_t_ref,
    window_ref,
    mix_ref,
    unmix_ref,
    back_ref,
    out_ref,
    mixed_ref,
    field_ref,
    aerial_ref,
    grad_ref,
    fold_ref,
    band_ref,
):
    corner = lax.axis_index("corner")
    tile = lax.axis_index("tile")
    edge = dot(edge_ref[:EDGE], forward_ref[...]).astype(BF)
    rows = jnp.concatenate([edge, spectra_ref[...]], axis=0)
    pick = picked(U, ROWS + EDGE, SHARE * corner + (EDGE - 2 * RIM))
    mask_hat = dot(window_ref[...], turned(dot(pick, rows))) * (1.0 / (TURN * TURN * TURN * U))
    mask_re = mask_hat[:, :LANES]
    mask_im = mask_hat[:, LANES:]
    for group in range(NFOC * NK // 4):
        parts = []
        for pair in range(2):
            stack = []
            for q in range(2):
                kernel = group * 4 + pair * 2 + q
                hat = hat_ref[(kernel % NK) * NFOC + kernel // NK].astype(F32)
                hat_re = hat[:, :LANES]
                hat_im = hat[:, LANES:]
                re = (mask_re * hat_re - mask_im * hat_im).astype(BF)
                im = (mask_re * hat_im + mask_im * hat_re).astype(BF)
                stack.append(jnp.concatenate([re, im], axis=1))
                stack.append(jnp.concatenate([-im, re], axis=1))
            parts.append(dot(mix_ref[...], jnp.concatenate(stack, axis=0)))
        mixed_ref[group * 4 * PAIR : (group + 1) * 4 * PAIR] = jnp.concatenate(parts, axis=0).astype(BF)
    per_focus = NK * PAIR
    fold_ref[...] = jnp.zeros_like(fold_ref)
    for focus in range(NFOC):
        fields = dot(mixed_ref[focus * per_focus : (focus + 1) * per_focus], inverse_ref[...])
        field_ref[focus * per_focus : (focus + 1) * per_focus] = fields
        power = fields[:, :GRID] * fields[:, :GRID] + fields[:, GRID:] * fields[:, GRID:]
        summed = power[: 2 * PAIR]
        for pair in range(1, NK // 2):
            summed = summed + power[pair * 2 * PAIR : (pair + 1) * 2 * PAIR]
        fold_ref[focus, : 2 * PAIR] = summed
        aerial_ref[focus * 24 : (focus + 1) * 24, :GRID] = (
            fold_ref[focus, 0:24] + fold_ref[focus, PAIR : PAIR + 24]
        )
    coarse = aerial_ref[:, :GRID]
    coarse_high = coarse.astype(BF)
    coarse_low = (coarse - coarse_high.astype(F32)).astype(BF)
    both = dot(jnp.concatenate([coarse_high, coarse_low], axis=0), interp_ref[...])
    aerial_ref[...] = both[: NFOC * 24] + both[NFOC * 24 :]
    wanted_rows = jnp.concatenate([edge_ref[EDGE:], target_ref[...].astype(F32).astype(BF)], axis=0)
    pick = picked(24, ROWS + TEDGE, SHARE * corner + (TEDGE - RIM))
    band_ref[...] = dot(pick, wanted_rows)
    local = lax.broadcasted_iota(jnp.int32, (24, ROWS), 0)
    pixel = tile * ROWS + SHARE * corner - RIM + local
    valid = (local < SHARE) & (pixel >= 0) & (pixel < ROWS * lax.axis_size("tile"))
    valid = jnp.where(valid, 1.0, 0.0)
    doses = [dose_ref[d : d + 1] for d in range(NDOSE)]
    for chunk in range(W // ROWS):
        cols = slice(chunk * ROWS, (chunk + 1) * ROWS)
        high = None
        low_sum = None
        kept = []
        for focus in range(NFOC):
            aerial = aerial_ref[focus * 24 : (focus + 1) * 24, cols]
            for d in range(NDOSE):
                swing = jnp.tanh((0.5 * STEEPNESS * doses[d]) * aerial - 0.5 * STEEPNESS * THRESHOLD)
                power = (0.5 * SHARPNESS / math.log(2.0)) * swing + 0.5 * SHARPNESS / math.log(2.0)
                up = jnp.exp2(power)
                down = jnp.exp2(-power)
                high = up if high is None else high + up
                low_sum = down if low_sum is None else low_sum + down
                kept.append((swing, up, down))
        wanted = band_ref[:, cols]
        top = jnp.log(high) / SHARPNESS
        bottom = -jnp.log(low_sum) / SHARPNESS
        band_ref[:, cols] = top - bottom
        high_weight = valid * (top - wanted) / high
        low_weight = valid * (bottom - wanted) / low_sum
        for focus in range(NFOC):
            total = None
            for d in range(NDOSE):
                swing, up, down = kept[focus * NDOSE + d]
                term = (high_weight * up + low_weight * down) * (1.0 - swing * swing)
                term = term * (0.5 * STEEPNESS * doses[d])
                total = term if total is None else total + term
            grad_ref[focus * 24 : (focus + 1) * 24, cols] = total
    coarse_grad = dot(grad_ref[...].astype(BF), interp_t_ref[...])
    acc_re = jnp.zeros((U, LANES), F32)
    acc_im = jnp.zeros((U, LANES), F32)
    for focus in range(NFOC):
        part = coarse_grad[focus * 24 : (focus + 1) * 24]
        fold_ref[focus, 0:24] = part
        fold_ref[focus, PAIR : PAIR + 24] = part
        twice = fold_ref[focus, : 2 * PAIR]
        twice = jnp.concatenate([twice, twice], axis=1)
        start = focus * per_focus
        field_grad = [
            (twice * field_ref[start + pair * 2 * PAIR : start + (pair + 1) * 2 * PAIR])
            for pair in range(NK // 2)
        ]
        mixed_grad = dot(jnp.concatenate(field_grad, axis=0).astype(BF), inverse_t_ref[...])
        for group in range(NK // 4):
            hats = dot(unmix_ref[...], turned(mixed_grad[group * 4 * PAIR : (group + 1) * 4 * PAIR]))
            for q in range(4):
                grad_re = hats[q * U : (q + 1) * U, :LANES]
                grad_im = hats[q * U : (q + 1) * U, LANES:]
                hat = hat_ref[(group * 4 + q) * NFOC + focus].astype(F32)
                hat_re = hat[:, :LANES]
                hat_im = hat[:, LANES:]
                acc_re = acc_re + (grad_re * hat_re + grad_im * hat_im)
                acc_im = acc_im + (grad_im * hat_re - grad_re * hat_im)
    acc = jnp.concatenate([acc_re, acc_im], axis=1) * (1.0 / (TURN * TURN * TURN * U))
    spectra_grad = dot(back_ref[...], turned(acc))
    mask_grad = dot(spectra_grad.astype(BF), forward_t_ref[...]).astype(BF)
    for block in range(W // ROWS):
        cols = slice(block * ROWS, (block + 1) * ROWS)
        out_ref[block, :U] = mask_grad[:, cols]
        band = jnp.concatenate([band_ref[:, cols], jnp.zeros((8, ROWS), F32)], axis=0)
        out_ref[block, U:] = band.astype(BF)


def finish_kernel(blocks_ref, slope_ref, place_grad_ref, place_band_ref, band_ref, grad_ref):
    count = blocks_ref.shape[0]
    grads = blocks_ref[:, :U].reshape(count * U, ROWS)
    grad_ref[...] = dot(place_grad_ref[...], grads) * slope_ref[...]
    bands = blocks_ref[:, U:].reshape(count * (MSG - U), ROWS)
    band_ref[...] = dot(place_band_ref[...], bands)


def params(mib):
    return pltpu.CompilerParams(vmem_limit_bytes=mib << 20)


def whole(count):
    return [pl.BlockSpec(memory_space=pltpu.VMEM)] * count


def per_device(mask_logits, target, kernels, dose_levels):
    tiles = lax.axis_size("tile")
    corners = lax.axis_size("corner")
    edge, dose_rows = pl.pallas_call(
        edge_kernel,
        name="edge",
        out_shape=(
            jax.ShapeDtypeStruct((EDGE + TEDGE, W), BF),
            jax.ShapeDtypeStruct((NDOSE, ROWS), F32),
        ),
        in_specs=[pl.BlockSpec(memory_space=pl.ANY)] * 3,
        out_specs=tuple(whole(2)),
        scratch_shapes=[
            pltpu.VMEM((EDGE, W), F32),
            pltpu.VMEM((TEDGE, W), jnp.int32),
            pltpu.SMEM((NDOSE,), F32),
            pltpu.SemaphoreType.DMA((3,)),
        ],
        compiler_params=params(2),
        cost_estimate=pl.CostEstimate(flops=2_000_000_000, bytes_accessed=0, transcendentals=0),
    )(*[pltpu.with_memory_space_constraint(x, pltpu.HBM) for x in (mask_logits, target, dose_levels)])
    pairs = []
    for i in range(tiles - 1):
        for c in range(corners):
            begin = SHARE * c - 2 * RIM
            if begin < 0:
                pairs.append((i * corners + c, (i + 1) * corners + c))
            elif begin + SHARE + 2 * RIM > ROWS:
                pairs.append(((i + 1) * corners + c, i * corners + c))
    edge = lax.ppermute(edge, ("tile", "corner"), pairs)
    forward = low(forward_table())
    inverse = low(inverse_table())
    interp = low(interpolation_table())
    count = NFOC * NK
    hats, spectra, slope = pl.pallas_call(
        prepare_kernel,
        name="prepare",
        out_shape=(
            jax.ShapeDtypeStruct((count, U, 2 * LANES), BF),
            jax.ShapeDtypeStruct((ROWS, 2 * LANES), BF),
            jax.ShapeDtypeStruct((ROWS, ROWS), F32),
        ),
        in_specs=whole(4),
        out_specs=tuple(whole(2)) + (pl.BlockSpec(memory_space=pltpu.HBM),),
        scratch_shapes=[
            pltpu.VMEM((2, TAP_ROWS, 2 * NF), F32),
            pltpu.VMEM((ROWS, ROWS), F32),
            pltpu.SemaphoreType.DMA,
        ],
        compiler_params=params(12),
        cost_estimate=pl.CostEstimate(flops=1_200_000_000, bytes_accessed=0, transcendentals=0),
    )(kernels.transpose(1, 2, 0, 3), mask_logits, forward, low(tap_table()))
    blocks = pl.pallas_call(
        image_kernel,
        name="image",
        out_shape=jax.ShapeDtypeStruct((W // ROWS, MSG, ROWS), BF),
        in_specs=whole(15),
        out_specs=pl.BlockSpec(memory_space=pltpu.VMEM),
        scratch_shapes=[
            pltpu.VMEM((count * PAIR, 2 * LANES), BF),
            pltpu.VMEM((count * PAIR, 2 * GRID), F32),
            pltpu.VMEM((NFOC * 24, W), F32),
            pltpu.VMEM((NFOC * 24, W), F32),
            pltpu.VMEM((NFOC, U, GRID), F32),
            pltpu.VMEM((24, W), F32),
        ],
        compiler_params=params(24),
        cost_estimate=pl.CostEstimate(flops=4_000_000_000, bytes_accessed=8_000_000, transcendentals=0),
    )(
        dose_rows,
        edge,
        spectra,
        target,
        hats,
        forward,
        inverse,
        interp,
        low(forward_table().T),
        low(inverse_table().T),
        low(interpolation_table().T),
        low(window_table()),
        low(mix_table()),
        low(unmix_table()),
        low(back_table()),
    )
    place_grad, place_band = placing_tables(corners)
    blocks = lax.all_to_all(blocks, "corner", 0, 0, tiled=True)
    return pl.pallas_call(
        finish_kernel,
        name="finish",
        out_shape=(
            jax.ShapeDtypeStruct((ROWS, ROWS), F32),
            jax.ShapeDtypeStruct((ROWS, ROWS), F32),
        ),
        in_specs=whole(4),
        out_specs=tuple(whole(2)),
        compiler_params=params(4),
    )(blocks, slope, low(place_grad), low(place_band))


def solution(mesh):
    return jax.shard_map(
        per_device,
        mesh=mesh,
        in_specs=(P("tile", None), P("tile", None), P(), P()),
        out_specs=(P("tile", "corner"), P("tile", "corner")),
        check_vma=False,
    )
```

```python
import math

import jax
import jax.numpy as jnp
import numpy as np
from jax import lax
from jax.experimental import pallas as pl
from jax.experimental.pallas import tpu as pltpu
from jax.sharding import PartitionSpec as P

STEEPNESS = 4.0
THRESHOLD = 1.0
SHARPNESS = 12.0

BF = jnp.bfloat16
F32 = jnp.float32

W = 1024
NF = 192
LANES = 256
TAPS = 25
RIM = TAPS // 2
ROWS = 128
NK = 12
NFOC = 4
NDOSE = 4
SHARE = 19
PAIR = 20
TAP_ROWS = 112
U = 48
GRID = 384
EDGE = 32
TEDGE = 16
MSG = 48 + 32
WINDOW = (0, 1, 7, 2, 6, 3, 4, 5)
TURN = 1.62425


def low(table):
    return jnp.asarray(np.asarray(table, np.float32)).astype(BF)


def forward_table():
    phase = np.outer(np.arange(NF) - NF // 2, np.arange(W)) % W
    angle = 2.0 * math.pi * phase / W
    scale = 1.0 / math.sqrt(W)
    table = np.zeros((W, 2 * LANES))
    table[:, :NF] = scale * np.cos(angle).T
    table[:, LANES : LANES + NF] = -scale * np.sin(angle).T
    return table


def inverse_table():
    phase = np.outer(np.arange(NF) - NF // 2, np.arange(GRID)) % GRID
    angle = 2.0 * math.pi * phase / GRID
    scale = 1.0 / math.sqrt(W)
    table = np.zeros((2 * LANES, 2 * GRID))
    table[:NF, :GRID] = scale * np.cos(angle)
    table[:NF, GRID:] = scale * np.sin(angle)
    table[LANES : LANES + NF, :GRID] = -scale * np.sin(angle)
    table[LANES : LANES + NF, GRID:] = scale * np.cos(angle)
    return table


def interpolation_table():
    where = np.arange(W)[None, :] / W - np.arange(GRID)[:, None] / GRID
    orders = np.arange(1, NF)
    table = np.ones((GRID, W))
    for order in orders:
        table += 2.0 * np.cos(2.0 * math.pi * order * where)
    return table / GRID


def row_angles(left, right):
    return 2.0 * math.pi * (np.outer(np.arange(left), np.arange(right)) % U) / U


def complex_table(angle):
    return TURN * np.block([[np.cos(angle), -np.sin(angle)], [np.sin(angle), np.cos(angle)]])


def tap_table():
    table = complex_table(row_angles(U, TAPS)).reshape(2, U, 2, TAPS)
    full = np.zeros((NFOC, 2, U, 2, TAP_ROWS))
    for focus in range(NFOC):
        full[focus, :, :, :, focus : TAPS * NFOC : NFOC] = table
    return full.reshape(NFOC * 2 * U, 2 * TAP_ROWS)


def window_table():
    return complex_table(-row_angles(U, U))


def back_table():
    angle = row_angles(U, U)
    return TURN * np.concatenate([np.cos(angle), np.sin(angle)], axis=1)


def mix_table(count=2):
    table = complex_table(row_angles(PAIR, U)).reshape(2, PAIR, 2, U)
    full = np.zeros((2, count, PAIR, count, 2, U))
    for q in range(count):
        full[:, q, :, q] = table
    return full.reshape(2 * count * PAIR, count * 2 * U)


def unmix_table(count=6):
    table = complex_table(-row_angles(U, PAIR)).reshape(2, U, 2, PAIR)
    full = np.zeros((count, 2, U, 2, count, PAIR))
    for q in range(count):
        full[q, :, :, :, q] = table
    return full.reshape(count * 2 * U, 2 * count * PAIR)


def entry_table():
    taps = tap_table()
    half = taps.shape[0] // 2
    table = np.zeros((W + half, 2 * LANES))
    table[:W] = forward_table()
    table[W:, : taps.shape[1]] = taps[:half]
    table[W:, LANES : LANES + taps.shape[1]] = taps[half:]
    return table


def row_tables():
    tables = [window_table(), mix_table(), unmix_table(), back_table()]
    places = []
    first = 0
    for table in tables:
        places.append((slice(first, first + table.shape[0]), slice(0, table.shape[1])))
        first += table.shape[0]
    whole_table = np.zeros((first, LANES))
    for table, place in zip(tables, places):
        whole_table[place] = table
    return whole_table, places


def placing_tables(count):
    grad = np.zeros((ROWS, count, U))
    band = np.zeros((ROWS, count, MSG - U))
    for source in range(count):
        for row in range(SHARE + 2 * RIM):
            pixel = SHARE * WINDOW[source] + row - 2 * RIM
            if 0 <= pixel < ROWS:
                grad[pixel, source, row] = 1.0
        for row in range(SHARE):
            pixel = SHARE * WINDOW[source] + row - RIM
            if 0 <= pixel < ROWS:
                band[pixel, source, row] = 1.0
    return grad.reshape(ROWS, -1), band.reshape(ROWS, -1)


def dot(left, right):
    return jnp.dot(left, right, preferred_element_type=F32)


def window_here():
    corner = lax.axis_index("corner")
    window = jnp.int32(WINDOW[0])
    for n in range(1, len(WINDOW)):
        window = jnp.where(corner == n, WINDOW[n], window)
    return window


def stacked(value):
    return jnp.concatenate([value[:, :LANES], value[:, LANES:]], axis=0).astype(BF)


def picked(count, length, first):
    row = lax.broadcasted_iota(jnp.int32, (count, length), 0) + first
    row = jnp.where(row >= length, row - length, row)
    column = lax.broadcasted_iota(jnp.int32, (count, length), 1)
    return jnp.where(row == column, 1.0, 0.0).astype(BF)


def edge_kernel(mask_ref, target_ref, dose_ref, out_ref, dose_rows_ref, mask_rows, target_rows, doses, sems):
    down = window_here() < len(WINDOW) // 2
    mask_from = pl.multiple_of(jnp.where(down, ROWS - EDGE, 0), EDGE)
    target_from = pl.multiple_of(jnp.where(down, ROWS - TEDGE, 0), TEDGE)
    copies = [
        pltpu.make_async_copy(mask_ref.at[pl.ds(mask_from, EDGE)], mask_rows, sems.at[0]),
        pltpu.make_async_copy(target_ref.at[pl.ds(target_from, TEDGE)], target_rows, sems.at[1]),
        pltpu.make_async_copy(dose_ref, doses, sems.at[2]),
    ]
    for copy in copies:
        copy.start()
    for copy in copies:
        copy.wait()
    out_ref[:EDGE] = jnp.tanh(mask_rows[...]).astype(BF)
    out_ref[EDGE:] = target_rows[...].astype(F32).astype(BF)
    for d in range(NDOSE):
        dose_rows_ref[d : d + 1] = jnp.full((1, ROWS), doses[d])


def prepare_kernel(
    kernels_ref, mask_ref, entry_ref, hat_ref, spectra_ref, slope_ref, taps_ref, share_ref, sem
):
    column = pl.multiple_of(lax.axis_index("corner") * ROWS, ROWS)
    share = jnp.tanh(mask_ref[:, pl.ds(column, ROWS)])
    share_ref[...] = 1.0 - share * share
    copy = pltpu.make_async_copy(share_ref, slope_ref, sem)
    copy.start()
    lane = lax.broadcasted_iota(jnp.int32, (TAP_ROWS, LANES), 1)
    taps_ref[:, :, NFOC * TAPS - 4 :] = jnp.zeros((2, 2, TAP_ROWS - NFOC * TAPS + 4, 2 * NF), F32)
    half = NFOC * U
    table = jnp.concatenate(
        [
            entry_ref[W : W + half, : 2 * TAP_ROWS],
            entry_ref[W : W + half, LANES : LANES + 2 * TAP_ROWS],
        ],
        axis=0,
    )
    for kernel in range(0, NK, 2):
        slot = kernel // 2 % 2
        parts = []
        for q in range(2):
            for tap in range(TAPS):
                taps_ref[slot, q, tap * NFOC : (tap + 1) * NFOC] = kernels_ref[kernel + q, tap]
            taps = taps_ref[slot, q]
            re = jnp.where(lane < NF, taps[:, :LANES], 0.0)
            im = jnp.where(lane < NF, pltpu.roll(taps, NF, 1)[:, :LANES], 0.0)
            parts.append(jnp.concatenate([re, im], axis=0).astype(BF))
        hats = dot(table, jnp.concatenate(parts, axis=1))
        for q in range(2):
            hat = hats[:, q * LANES : (q + 1) * LANES].reshape(NFOC, 2 * U, LANES)
            hat_ref[(kernel + q) * NFOC : (kernel + q + 1) * NFOC] = hat
    field = jnp.tanh(mask_ref[...])
    spectra_ref[...] = dot(field.astype(BF), entry_ref[:W]).astype(BF)
    copy.wait()


def image_kernel(
    dose_ref,
    edge_ref,
    spectra_ref,
    target_ref,
    hat_ref,
    entry_ref,
    inverse_ref,
    interp_ref,
    forward_t_ref,
    inverse_t_ref,
    interp_t_ref,
    rows_ref,
    out_ref,
    mixed_ref,
    field_ref,
    aerial_ref,
    grad_ref,
    fold_ref,
    band_ref,
):
    window = window_here()
    tile = lax.axis_index("tile")
    window_rows, mix_rows, unmix_rows, back_rows = row_tables()[1]
    edge = dot(edge_ref[:EDGE], entry_ref[:W]).astype(BF)
    rows = jnp.concatenate([edge, spectra_ref[...]], axis=0)
    pick = picked(U, ROWS + EDGE, SHARE * window + (EDGE - 2 * RIM))
    mask_hat = dot(rows_ref[window_rows], stacked(dot(pick, rows))) * (1.0 / (TURN * TURN * TURN * U))
    mask_re = mask_hat[:U]
    mask_im = mask_hat[U:]
    for group in range(NFOC * NK // 4):
        stacks = []
        for pair in range(2):
            stack = []
            for q in range(2):
                kernel = group * 4 + pair * 2 + q
                hat = hat_ref[(kernel % NK) * NFOC + kernel // NK]
                stack.append(mask_re * hat[:U] - mask_im * hat[U:])
                stack.append(mask_re * hat[U:] + mask_im * hat[:U])
            stacks.append(jnp.concatenate(stack, axis=0).astype(BF))
        mixed = dot(rows_ref[mix_rows], jnp.concatenate(stacks, axis=1))
        parts = []
        for pair in range(2):
            lanes = slice(pair * LANES, (pair + 1) * LANES)
            parts.append(jnp.concatenate([mixed[: 2 * PAIR, lanes], mixed[2 * PAIR :, lanes]], axis=1))
        mixed_ref[group * 4 * PAIR : (group + 1) * 4 * PAIR] = jnp.concatenate(parts, axis=0).astype(BF)
    per_focus = NK * PAIR
    fold_ref[...] = jnp.zeros_like(fold_ref)
    for focus in range(NFOC):
        fields = dot(mixed_ref[focus * per_focus : (focus + 1) * per_focus], inverse_ref[...])
        field_ref[focus * per_focus : (focus + 1) * per_focus] = fields
        power = fields[:, :GRID] * fields[:, :GRID] + fields[:, GRID:] * fields[:, GRID:]
        summed = power[: 2 * PAIR]
        for pair in range(1, NK // 2):
            summed = summed + power[pair * 2 * PAIR : (pair + 1) * 2 * PAIR]
        fold_ref[focus, : 2 * PAIR] = summed
        aerial_ref[focus * 24 : (focus + 1) * 24, :GRID] = (
            fold_ref[focus, 0:24] + fold_ref[focus, PAIR : PAIR + 24]
        )
    coarse = aerial_ref[:, :GRID]
    coarse_high = coarse.astype(BF)
    coarse_low = (coarse - coarse_high.astype(F32)).astype(BF)
    both = dot(jnp.concatenate([coarse_high, coarse_low], axis=0), interp_ref[...])
    aerial_ref[...] = both[: NFOC * 24] + both[NFOC * 24 :]
    wanted_rows = jnp.concatenate([edge_ref[EDGE:], target_ref[...].astype(F32).astype(BF)], axis=0)
    pick = picked(24, ROWS + TEDGE, SHARE * window + (TEDGE - RIM))
    band_ref[...] = dot(pick, wanted_rows)
    local = lax.broadcasted_iota(jnp.int32, (24, ROWS), 0)
    pixel = tile * ROWS + SHARE * window - RIM + local
    valid = (local < SHARE) & (pixel >= 0) & (pixel < ROWS * lax.axis_size("tile"))
    valid = jnp.where(valid, 1.0, 0.0)
    doses = [dose_ref[d : d + 1] for d in range(NDOSE)]
    for chunk in range(W // ROWS):
        cols = slice(chunk * ROWS, (chunk + 1) * ROWS)
        high = None
        low_sum = None
        kept = []
        for focus in range(NFOC):
            aerial = aerial_ref[focus * 24 : (focus + 1) * 24, cols]
            for d in range(NDOSE):
                swing = jnp.tanh((0.5 * STEEPNESS * doses[d]) * aerial - 0.5 * STEEPNESS * THRESHOLD)
                power = (0.5 * SHARPNESS / math.log(2.0)) * swing + 0.5 * SHARPNESS / math.log(2.0)
                up = jnp.exp2(power)
                down = jnp.exp2(-power)
                high = up if high is None else high + up
                low_sum = down if low_sum is None else low_sum + down
                kept.append((swing, up, down))
        wanted = band_ref[:, cols]
        top = jnp.log(high) / SHARPNESS
        bottom = -jnp.log(low_sum) / SHARPNESS
        band_ref[:, cols] = top - bottom
        high_weight = valid * (top - wanted) / high
        low_weight = valid * (bottom - wanted) / low_sum
        for focus in range(NFOC):
            total = None
            for d in range(NDOSE):
                swing, up, down = kept[focus * NDOSE + d]
                term = (high_weight * up + low_weight * down) * (1.0 - swing * swing)
                term = term * (0.5 * STEEPNESS * doses[d])
                total = term if total is None else total + term
            grad_ref[focus * 24 : (focus + 1) * 24, cols] = total
    coarse_grad = dot(grad_ref[...].astype(BF), interp_t_ref[...])
    acc_re = jnp.zeros((U, LANES), F32)
    acc_im = jnp.zeros((U, LANES), F32)
    for focus in range(NFOC):
        part = coarse_grad[focus * 24 : (focus + 1) * 24]
        fold_ref[focus, 0:24] = part
        fold_ref[focus, PAIR : PAIR + 24] = part
        twice = fold_ref[focus, : 2 * PAIR]
        twice = jnp.concatenate([twice, twice], axis=1)
        start = focus * per_focus
        field_grad = [
            (twice * field_ref[start + pair * 2 * PAIR : start + (pair + 1) * 2 * PAIR])
            for pair in range(NK // 2)
        ]
        mixed_grad = dot(jnp.concatenate(field_grad, axis=0).astype(BF), inverse_t_ref[...])
        grads = [stacked(mixed_grad[group * 6 * PAIR : (group + 1) * 6 * PAIR]) for group in range(NK // 6)]
        grads = dot(rows_ref[unmix_rows], jnp.concatenate(grads, axis=1))
        for group in range(NK // 6):
            lanes = slice(group * LANES, (group + 1) * LANES)
            for q in range(6):
                grad_re = grads[2 * q * U : (2 * q + 1) * U, lanes]
                grad_im = grads[(2 * q + 1) * U : (2 * q + 2) * U, lanes]
                hat = hat_ref[(group * 6 + q) * NFOC + focus]
                acc_re = acc_re + (grad_re * hat[:U] + grad_im * hat[U:])
                acc_im = acc_im + (grad_im * hat[:U] - grad_re * hat[U:])
    acc_re = acc_re * (1.0 / (TURN * TURN * TURN * U))
    acc_im = acc_im * (1.0 / (TURN * TURN * TURN * U))
    acc = jnp.concatenate(
        [jnp.concatenate([acc_re, acc_im], axis=1), jnp.concatenate([-acc_im, acc_re], axis=1)], axis=0
    )
    spectra_grad = dot(rows_ref[back_rows], acc.astype(BF))
    mask_grad = dot(spectra_grad.astype(BF), forward_t_ref[...]).astype(BF)
    for block in range(W // ROWS):
        cols = slice(block * ROWS, (block + 1) * ROWS)
        out_ref[block, :U] = mask_grad[:, cols]
        band = jnp.concatenate([band_ref[:, cols], jnp.zeros((8, ROWS), F32)], axis=0)
        out_ref[block, U:] = band.astype(BF)


def finish_kernel(blocks_ref, slope_ref, place_grad_ref, place_band_ref, band_ref, grad_ref):
    count = blocks_ref.shape[0]
    grads = blocks_ref[:, :U].reshape(count * U, ROWS)
    grad_ref[...] = dot(place_grad_ref[...], grads) * slope_ref[...]
    bands = blocks_ref[:, U:].reshape(count * (MSG - U), ROWS)
    band_ref[...] = dot(place_band_ref[...], bands)


def params(mib):
    return pltpu.CompilerParams(vmem_limit_bytes=mib << 20)


def whole(count):
    return [pl.BlockSpec(memory_space=pltpu.VMEM)] * count


def per_device(mask_logits, target, kernels, dose_levels):
    tiles = lax.axis_size("tile")
    corners = lax.axis_size("corner")
    edge, dose_rows = pl.pallas_call(
        edge_kernel,
        name="edge",
        out_shape=(
            jax.ShapeDtypeStruct((EDGE + TEDGE, W), BF),
            jax.ShapeDtypeStruct((NDOSE, ROWS), F32),
        ),
        in_specs=[pl.BlockSpec(memory_space=pl.ANY)] * 3,
        out_specs=tuple(whole(2)),
        scratch_shapes=[
            pltpu.VMEM((EDGE, W), F32),
            pltpu.VMEM((TEDGE, W), jnp.int32),
            pltpu.SMEM((NDOSE,), F32),
            pltpu.SemaphoreType.DMA((3,)),
        ],
        compiler_params=params(2),
        cost_estimate=pl.CostEstimate(flops=2_000_000_000, bytes_accessed=0, transcendentals=0),
    )(*[pltpu.with_memory_space_constraint(x, pltpu.HBM) for x in (mask_logits, target, dose_levels)])
    pairs = []
    for i in range(tiles - 1):
        for c in range(corners):
            begin = SHARE * WINDOW[c] - 2 * RIM
            if begin < 0:
                pairs.append((i * corners + c, (i + 1) * corners + c))
            elif begin + SHARE + 2 * RIM > ROWS:
                pairs.append(((i + 1) * corners + c, i * corners + c))
    edge = lax.ppermute(edge, ("tile", "corner"), pairs)
    entry = low(entry_table())
    inverse = low(inverse_table())
    interp = low(interpolation_table())
    count = NFOC * NK
    hats, spectra, slope = pl.pallas_call(
        prepare_kernel,
        name="prepare",
        out_shape=(
            jax.ShapeDtypeStruct((count, 2 * U, LANES), F32),
            jax.ShapeDtypeStruct((ROWS, 2 * LANES), BF),
            jax.ShapeDtypeStruct((ROWS, ROWS), F32),
        ),
        in_specs=whole(3),
        out_specs=tuple(whole(2)) + (pl.BlockSpec(memory_space=pltpu.HBM),),
        scratch_shapes=[
            pltpu.VMEM((2, 2, TAP_ROWS, 2 * NF), F32),
            pltpu.VMEM((ROWS, ROWS), F32),
            pltpu.SemaphoreType.DMA,
        ],
        compiler_params=params(6),
        cost_estimate=pl.CostEstimate(flops=1_200_000_000, bytes_accessed=0, transcendentals=0),
    )(kernels.transpose(1, 2, 0, 3), mask_logits, entry)
    blocks = pl.pallas_call(
        image_kernel,
        name="image",
        out_shape=jax.ShapeDtypeStruct((W // ROWS, MSG, ROWS), BF),
        in_specs=whole(12),
        out_specs=pl.BlockSpec(memory_space=pltpu.VMEM),
        scratch_shapes=[
            pltpu.VMEM((count * PAIR, 2 * LANES), BF),
            pltpu.VMEM((count * PAIR, 2 * GRID), F32),
            pltpu.VMEM((NFOC * 24, W), F32),
            pltpu.VMEM((NFOC * 24, W), F32),
            pltpu.VMEM((NFOC, U, GRID), F32),
            pltpu.VMEM((24, W), F32),
        ],
        compiler_params=params(14),
        cost_estimate=pl.CostEstimate(flops=4_000_000_000, bytes_accessed=8_000_000, transcendentals=0),
    )(
        dose_rows,
        edge,
        spectra,
        target,
        hats,
        entry,
        inverse,
        interp,
        low(forward_table().T),
        low(inverse_table().T),
        low(interpolation_table().T),
        low(row_tables()[0]),
    )
    place_grad, place_band = placing_tables(corners)
    blocks = lax.all_to_all(blocks, "corner", 0, 0, tiled=True)
    return pl.pallas_call(
        finish_kernel,
        name="finish",
        out_shape=(
            jax.ShapeDtypeStruct((ROWS, ROWS), F32),
            jax.ShapeDtypeStruct((ROWS, ROWS), F32),
        ),
        in_specs=whole(4),
        out_specs=tuple(whole(2)),
        compiler_params=params(4),
    )(blocks, slope, low(place_grad), low(place_band))


def solution(mesh):
    return jax.shard_map(
        per_device,
        mesh=mesh,
        in_specs=(P("tile", None), P("tile", None), P(), P()),
        out_specs=(P("tile", "corner"), P("tile", "corner")),
        check_vma=False,
    )
```

```python
import math

import jax
import jax.numpy as jnp
import numpy as np
from jax import lax
from jax.experimental import pallas as pl
from jax.experimental.pallas import tpu as pltpu
from jax.sharding import PartitionSpec as P

STEEPNESS = 4.0
THRESHOLD = 1.0
SHARPNESS = 12.0

BF = jnp.bfloat16
F32 = jnp.float32

W = 1024
NF = 192
LANES = 256
TAPS = 25
RIM = TAPS // 2
ROWS = 128
NK = 12
NFOC = 4
NDOSE = 4
TAP_ROWS = 112
GRID = 384
EDGE = 32
TEDGE = 16
GRAD_ROWS = 48
BAND_ROWS = 32


class Plan:
    def __init__(self, share, rows, order, turn):
        self.share = share
        self.rows = rows
        self.order = order
        self.turn = turn


OUTER = Plan(14, 16, 40, 1.91284375)
INNER = Plan(24, 24, 48, 1.62425)
PLANS = (OUTER, OUTER, INNER, INNER, INNER, INNER, OUTER, OUTER)
STARTS = tuple(sum(plan.share for plan in PLANS[:n]) - RIM for n in range(len(PLANS)))
WINDOW = (0, 1, 7, 2, 6, 3, 4, 5)


def low(table):
    return jnp.asarray(np.asarray(table, np.float32)).astype(BF)


def forward_table():
    phase = np.outer(np.arange(NF) - NF // 2, np.arange(W)) % W
    angle = 2.0 * math.pi * phase / W
    scale = 1.0 / math.sqrt(W)
    table = np.zeros((W, 2 * LANES))
    table[:, :NF] = scale * np.cos(angle).T
    table[:, LANES : LANES + NF] = -scale * np.sin(angle).T
    return table


def inverse_table():
    phase = np.outer(np.arange(NF) - NF // 2, np.arange(GRID)) % GRID
    angle = 2.0 * math.pi * phase / GRID
    scale = 1.0 / math.sqrt(W)
    table = np.zeros((2 * LANES, 2 * GRID))
    table[:NF, :GRID] = scale * np.cos(angle)
    table[:NF, GRID:] = scale * np.sin(angle)
    table[LANES : LANES + NF, :GRID] = -scale * np.sin(angle)
    table[LANES : LANES + NF, GRID:] = scale * np.cos(angle)
    return table


def interpolation_table():
    where = np.arange(W)[None, :] / W - np.arange(GRID)[:, None] / GRID
    orders = np.arange(1, NF)
    table = np.ones((GRID, W))
    for order in orders:
        table += 2.0 * np.cos(2.0 * math.pi * order * where)
    return table / GRID


def row_angles(order, left, right):
    return 2.0 * math.pi * (np.outer(np.arange(left), np.arange(right)) % order) / order


def complex_table(plan, angle):
    return plan.turn * np.block([[np.cos(angle), -np.sin(angle)], [np.sin(angle), np.cos(angle)]])


def tap_table(plan):
    u = plan.order
    table = complex_table(plan, row_angles(u, u, TAPS)).reshape(2, u, 2, TAPS)
    full = np.zeros((NFOC, 2, u, 2, TAP_ROWS))
    for focus in range(NFOC):
        full[focus, :, :, :, focus : TAPS * NFOC : NFOC] = table
    return full.reshape(NFOC * 2 * u, 2 * TAP_ROWS)


def window_table(plan):
    return complex_table(plan, -row_angles(plan.order, plan.order, plan.order))


def back_table(plan):
    angle = row_angles(plan.order, plan.order, plan.order)
    return plan.turn * np.concatenate([np.cos(angle), np.sin(angle)], axis=1)


def mix_table(plan, count=2):
    u, rows = plan.order, plan.rows
    table = complex_table(plan, row_angles(u, rows, u)).reshape(2, rows, 2, u)
    full = np.zeros((2, count, rows, count, 2, u))
    for q in range(count):
        full[:, q, :, q] = table
    return full.reshape(2 * count * rows, count * 2 * u)


def unmix_table(plan, count=4):
    u, rows = plan.order, plan.rows
    table = complex_table(plan, -row_angles(u, u, rows)).reshape(2, u, 2, rows)
    full = np.zeros((count, 2, u, 2, count, rows))
    for q in range(count):
        full[q, :, :, :, q] = table
    return full.reshape(count * 2 * u, 2 * count * rows)


def entry_table():
    parts = [forward_table()]
    places = {}
    first = W
    for plan in (INNER, OUTER):
        taps = tap_table(plan)
        half, width = taps.shape[0] // 2, taps.shape[1]
        part = np.zeros((half, 2 * LANES))
        part[:, :width] = taps[:half]
        part[:, LANES : LANES + width] = taps[half:]
        parts.append(part)
        places[plan] = slice(first, first + half)
        first += half
    return np.concatenate(parts), places


def row_tables():
    places = {}
    parts = []
    first = 0
    for plan in (INNER, OUTER):
        places[plan] = []
        for table in (window_table(plan), mix_table(plan), unmix_table(plan), back_table(plan)):
            rows, width = table.shape
            places[plan].append((slice(first, first + rows), slice(0, width)))
            part = np.zeros((-(-rows // 16) * 16, LANES))
            part[:rows, :width] = table
            parts.append(part)
            first += part.shape[0]
    return np.concatenate(parts), places


def placing_tables(count):
    grad = np.zeros((ROWS, count, GRAD_ROWS))
    band = np.zeros((ROWS, count, BAND_ROWS))
    for source in range(count):
        share, start = PLANS[WINDOW[source]].share, STARTS[WINDOW[source]]
        for row in range(share + 2 * RIM):
            if 0 <= start - RIM + row < ROWS:
                grad[start - RIM + row, source, row] = 1.0
        for row in range(share):
            if 0 <= start + row < ROWS:
                band[start + row, source, row] = 1.0
    return grad.reshape(ROWS, -1), band.reshape(ROWS, -1)


def dot(left, right):
    return jnp.dot(left, right, preferred_element_type=F32)


def here(values):
    corner = lax.axis_index("corner")
    value = jnp.int32(values[WINDOW[0]])
    for n in range(1, len(WINDOW)):
        value = jnp.where(corner == n, values[WINDOW[n]], value)
    return value


def by_plan(work):
    outer = here([int(plan is OUTER) for plan in PLANS]) == 1
    pl.when(outer)(lambda: work(OUTER))
    pl.when(jnp.logical_not(outer))(lambda: work(INNER))


def stacked(value):
    return jnp.concatenate([value[:, :LANES], value[:, LANES:]], axis=0).astype(BF)


def picked(count, length, first):
    row = lax.broadcasted_iota(jnp.int32, (count, length), 0) + first
    row = jnp.where(row >= length, row - length, row)
    column = lax.broadcasted_iota(jnp.int32, (count, length), 1)
    return jnp.where(row == column, 1.0, 0.0).astype(BF)


def edge_kernel(mask_ref, target_ref, dose_ref, out_ref, dose_rows_ref, mask_rows, target_rows, doses, sems):
    down = here(range(len(WINDOW))) < len(WINDOW) // 2
    mask_from = pl.multiple_of(jnp.where(down, ROWS - EDGE, 0), EDGE)
    target_from = pl.multiple_of(jnp.where(down, ROWS - TEDGE, 0), TEDGE)
    copies = [
        pltpu.make_async_copy(mask_ref.at[pl.ds(mask_from, EDGE)], mask_rows, sems.at[0]),
        pltpu.make_async_copy(target_ref.at[pl.ds(target_from, TEDGE)], target_rows, sems.at[1]),
        pltpu.make_async_copy(dose_ref, doses, sems.at[2]),
    ]
    for copy in copies:
        copy.start()
    for copy in copies:
        copy.wait()
    out_ref[:EDGE] = jnp.tanh(mask_rows[...]).astype(BF)
    out_ref[EDGE:] = target_rows[...].astype(F32).astype(BF)
    for d in range(NDOSE):
        dose_rows_ref[d : d + 1] = jnp.full((1, ROWS), doses[d])


def prepare_kernel(kernels_ref, mask_ref, entry_ref, hat_ref, spectra_ref, slope_ref, taps_ref, share_ref, sem):
    column = pl.multiple_of(lax.axis_index("corner") * ROWS, ROWS)
    share = jnp.tanh(mask_ref[:, pl.ds(column, ROWS)])
    share_ref[...] = 1.0 - share * share
    copy = pltpu.make_async_copy(share_ref, slope_ref, sem)
    copy.start()
    taps_ref[:, :, NFOC * TAPS - 4 :] = jnp.zeros((2, 2, TAP_ROWS - NFOC * TAPS + 4, 2 * NF), F32)
    places = entry_table()[1]

    def transform(plan):
        u = plan.order
        lane = lax.broadcasted_iota(jnp.int32, (TAP_ROWS, LANES), 1)
        table = jnp.concatenate(
            [
                entry_ref[places[plan], : 2 * TAP_ROWS],
                entry_ref[places[plan], LANES : LANES + 2 * TAP_ROWS],
            ],
            axis=0,
        )
        for kernel in range(0, NK, 2):
            slot = kernel // 2 % 2
            parts = []
            for q in range(2):
                for tap in range(TAPS):
                    taps_ref[slot, q, tap * NFOC : (tap + 1) * NFOC] = kernels_ref[kernel + q, tap]
                taps = taps_ref[slot, q]
                re = jnp.where(lane < NF, taps[:, :LANES], 0.0)
                im = jnp.where(lane < NF, pltpu.roll(taps, NF, 1)[:, :LANES], 0.0)
                parts.append(jnp.concatenate([re, im], axis=0).astype(BF))
            hats = dot(table, jnp.concatenate(parts, axis=1))
            for q in range(2):
                hat = hats[:, q * LANES : (q + 1) * LANES].reshape(NFOC, 2 * u, LANES)
                hat_ref[(kernel + q) * NFOC : (kernel + q + 1) * NFOC, : 2 * u] = hat

    by_plan(transform)
    field = jnp.tanh(mask_ref[...])
    spectra_ref[...] = dot(field.astype(BF), entry_ref[:W]).astype(BF)
    copy.wait()


def image_kernel(
    dose_ref,
    edge_ref,
    spectra_ref,
    target_ref,
    hat_ref,
    entry_ref,
    inverse_ref,
    interp_ref,
    forward_t_ref,
    inverse_t_ref,
    interp_t_ref,
    rows_ref,
    out_ref,
    mixed_ref,
    field_ref,
    aerial_ref,
    grad_ref,
    band_ref,
):
    places = row_tables()[1]

    def work(plan):
        u, count = plan.order, plan.rows
        scale = 1.0 / (plan.turn * plan.turn * plan.turn * u)
        window_rows, mix_rows, unmix_rows, back_rows = places[plan]
        start = here(STARTS)
        rows = spectra_ref[...]
        wanted = target_ref[...].astype(F32).astype(BF)
        first, first_wanted = start - RIM, start
        if plan is OUTER:
            rows = jnp.concatenate([dot(edge_ref[:EDGE], entry_ref[:W]).astype(BF), rows], axis=0)
            wanted = jnp.concatenate([edge_ref[EDGE:], wanted], axis=0)
            first, first_wanted = first + EDGE, first_wanted + TEDGE
        pick = picked(u, rows.shape[0], first)
        mask_hat = dot(rows_ref[window_rows], stacked(dot(pick, rows))) * scale
        mask_re = mask_hat[:u]
        mask_im = mask_hat[u:]
        band_ref[:count] = dot(picked(count, wanted.shape[0], first_wanted), wanted)
        for group in range(NFOC * NK // 4):
            stacks = []
            for pair in range(2):
                stack = []
                for q in range(2):
                    kernel = group * 4 + pair * 2 + q
                    hat = hat_ref[(kernel % NK) * NFOC + kernel // NK, : 2 * u]
                    stack.append(mask_re * hat[:u] - mask_im * hat[u:])
                    stack.append(mask_re * hat[u:] + mask_im * hat[:u])
                stacks.append(jnp.concatenate(stack, axis=0).astype(BF))
            mixed = dot(rows_ref[mix_rows], jnp.concatenate(stacks, axis=1))
            parts = []
            for pair in range(2):
                lanes = slice(pair * LANES, (pair + 1) * LANES)
                parts.append(jnp.concatenate([mixed[: 2 * count, lanes], mixed[2 * count :, lanes]], axis=1))
            mixed_ref[group * 4 * count : (group + 1) * 4 * count] = jnp.concatenate(parts, axis=0).astype(BF)
        per_focus = NK * count
        coarse = []
        for focus in range(NFOC):
            fields = dot(mixed_ref[focus * per_focus : (focus + 1) * per_focus], inverse_ref[...])
            field_ref[focus * per_focus : (focus + 1) * per_focus] = fields
            power = fields[:, :GRID] * fields[:, :GRID] + fields[:, GRID:] * fields[:, GRID:]
            summed = power[:count]
            for kernel in range(1, NK):
                summed = summed + power[kernel * count : (kernel + 1) * count]
            coarse.append(summed)
        coarse = jnp.concatenate(coarse, axis=0)
        coarse_high = coarse.astype(BF)
        coarse_low = (coarse - coarse_high.astype(F32)).astype(BF)
        both = dot(jnp.concatenate([coarse_high, coarse_low], axis=0), interp_ref[...])
        aerial_ref[: NFOC * count] = both[: NFOC * count] + both[NFOC * count :]
        local = lax.broadcasted_iota(jnp.int32, (count, ROWS), 0)
        pixel = lax.axis_index("tile") * ROWS + start + local
        valid = (local < plan.share) & (pixel >= 0) & (pixel < ROWS * lax.axis_size("tile"))
        valid = jnp.where(valid, 1.0, 0.0)
        doses = [dose_ref[d : d + 1] for d in range(NDOSE)]
        for chunk in range(W // ROWS):
            cols = slice(chunk * ROWS, (chunk + 1) * ROWS)
            high = None
            low_sum = None
            kept = []
            for focus in range(NFOC):
                aerial = aerial_ref[focus * count : (focus + 1) * count, cols]
                for d in range(NDOSE):
                    swing = jnp.tanh((0.5 * STEEPNESS * doses[d]) * aerial - 0.5 * STEEPNESS * THRESHOLD)
                    power = (0.5 * SHARPNESS / math.log(2.0)) * swing + 0.5 * SHARPNESS / math.log(2.0)
                    up = jnp.exp2(power)
                    down = jnp.exp2(-power)
                    high = up if high is None else high + up
                    low_sum = down if low_sum is None else low_sum + down
                    kept.append((swing, up, down))
            pixels = band_ref[:count, cols]
            top = jnp.log(high) / SHARPNESS
            bottom = -jnp.log(low_sum) / SHARPNESS
            band_ref[:count, cols] = top - bottom
            high_weight = valid * (top - pixels) / high
            low_weight = valid * (bottom - pixels) / low_sum
            for focus in range(NFOC):
                total = None
                for d in range(NDOSE):
                    swing, up, down = kept[focus * NDOSE + d]
                    term = (high_weight * up + low_weight * down) * (1.0 - swing * swing)
                    term = term * (0.5 * STEEPNESS * doses[d])
                    total = term if total is None else total + term
                grad_ref[focus * count : (focus + 1) * count, cols] = total
        coarse_grad = dot(grad_ref[: NFOC * count].astype(BF), interp_t_ref[...])
        acc_re = jnp.zeros((u, LANES), F32)
        acc_im = jnp.zeros((u, LANES), F32)
        for focus in range(NFOC):
            part = coarse_grad[focus * count : (focus + 1) * count]
            part = jnp.concatenate([part, part], axis=1)
            base = focus * per_focus
            field_grad = [
                part * field_ref[base + kernel * count : base + (kernel + 1) * count] for kernel in range(NK)
            ]
            mixed_grad = dot(jnp.concatenate(field_grad, axis=0).astype(BF), inverse_t_ref[...])
            grads = [
                stacked(mixed_grad[group * 4 * count : (group + 1) * 4 * count]) for group in range(NK // 4)
            ]
            grads = dot(rows_ref[unmix_rows], jnp.concatenate(grads, axis=1))
            for group in range(NK // 4):
                lanes = slice(group * LANES, (group + 1) * LANES)
                for q in range(4):
                    grad_re = grads[2 * q * u : (2 * q + 1) * u, lanes]
                    grad_im = grads[(2 * q + 1) * u : (2 * q + 2) * u, lanes]
                    hat = hat_ref[(group * 4 + q) * NFOC + focus, : 2 * u]
                    acc_re = acc_re + (grad_re * hat[:u] + grad_im * hat[u:])
                    acc_im = acc_im + (grad_im * hat[:u] - grad_re * hat[u:])
        acc_re = acc_re * scale
        acc_im = acc_im * scale
        acc = jnp.concatenate(
            [jnp.concatenate([acc_re, acc_im], axis=1), jnp.concatenate([-acc_im, acc_re], axis=1)], axis=0
        )
        spectra_grad = dot(rows_ref[back_rows], acc.astype(BF))
        if u < GRAD_ROWS:
            spectra_grad = jnp.concatenate([spectra_grad, jnp.zeros((GRAD_ROWS - u, 2 * LANES), F32)], axis=0)
        mask_grad = dot(spectra_grad.astype(BF), forward_t_ref[...]).astype(BF)
        empty = jnp.zeros((BAND_ROWS - count, ROWS), F32)
        for block in range(W // ROWS):
            cols = slice(block * ROWS, (block + 1) * ROWS)
            out_ref[block, :GRAD_ROWS] = mask_grad[:, cols]
            out_ref[block, GRAD_ROWS:] = jnp.concatenate([band_ref[:count, cols], empty], axis=0).astype(BF)

    by_plan(work)


def finish_kernel(blocks_ref, slope_ref, place_grad_ref, place_band_ref, band_ref, grad_ref):
    count = blocks_ref.shape[0]
    grads = blocks_ref[:, :GRAD_ROWS].reshape(count * GRAD_ROWS, ROWS)
    grad_ref[...] = dot(place_grad_ref[...], grads) * slope_ref[...]
    bands = blocks_ref[:, GRAD_ROWS:].reshape(count * BAND_ROWS, ROWS)
    band_ref[...] = dot(place_band_ref[...], bands)


def params(mib):
    return pltpu.CompilerParams(vmem_limit_bytes=mib << 20)


def whole(count):
    return [pl.BlockSpec(memory_space=pltpu.VMEM)] * count


def per_device(mask_logits, target, kernels, dose_levels):
    tiles = lax.axis_size("tile")
    corners = lax.axis_size("corner")
    edge, dose_rows = pl.pallas_call(
        edge_kernel,
        name="edge",
        out_shape=(
            jax.ShapeDtypeStruct((EDGE + TEDGE, W), BF),
            jax.ShapeDtypeStruct((NDOSE, ROWS), F32),
        ),
        in_specs=[pl.BlockSpec(memory_space=pl.ANY)] * 3,
        out_specs=tuple(whole(2)),
        scratch_shapes=[
            pltpu.VMEM((EDGE, W), F32),
            pltpu.VMEM((TEDGE, W), jnp.int32),
            pltpu.SMEM((NDOSE,), F32),
            pltpu.SemaphoreType.DMA((3,)),
        ],
        compiler_params=params(2),
        cost_estimate=pl.CostEstimate(flops=2_000_000_000, bytes_accessed=0, transcendentals=0),
    )(*[pltpu.with_memory_space_constraint(x, pltpu.HBM) for x in (mask_logits, target, dose_levels)])
    pairs = []
    for i in range(tiles - 1):
        for c in range(corners):
            begin = STARTS[WINDOW[c]] - RIM
            if begin < 0:
                pairs.append((i * corners + c, (i + 1) * corners + c))
            elif begin + PLANS[WINDOW[c]].share + 2 * RIM > ROWS:
                pairs.append(((i + 1) * corners + c, i * corners + c))
    edge = lax.ppermute(edge, ("tile", "corner"), pairs)
    entry = low(entry_table()[0])
    inverse = low(inverse_table())
    interp = low(interpolation_table())
    count = NFOC * NK
    hats, spectra, slope = pl.pallas_call(
        prepare_kernel,
        name="prepare",
        out_shape=(
            jax.ShapeDtypeStruct((count, 2 * INNER.order, LANES), F32),
            jax.ShapeDtypeStruct((ROWS, 2 * LANES), BF),
            jax.ShapeDtypeStruct((ROWS, ROWS), F32),
        ),
        in_specs=whole(3),
        out_specs=tuple(whole(2)) + (pl.BlockSpec(memory_space=pltpu.HBM),),
        scratch_shapes=[
            pltpu.VMEM((2, 2, TAP_ROWS, 2 * NF), F32),
            pltpu.VMEM((ROWS, ROWS), F32),
            pltpu.SemaphoreType.DMA,
        ],
        compiler_params=params(6),
        cost_estimate=pl.CostEstimate(flops=1_200_000_000, bytes_accessed=0, transcendentals=0),
    )(kernels.transpose(1, 2, 0, 3), mask_logits, entry)
    blocks = pl.pallas_call(
        image_kernel,
        name="image",
        out_shape=jax.ShapeDtypeStruct((W // ROWS, GRAD_ROWS + BAND_ROWS, ROWS), BF),
        in_specs=whole(12),
        out_specs=pl.BlockSpec(memory_space=pltpu.VMEM),
        scratch_shapes=[
            pltpu.VMEM((count * INNER.rows, 2 * LANES), BF),
            pltpu.VMEM((count * INNER.rows, 2 * GRID), F32),
            pltpu.VMEM((NFOC * INNER.rows, W), F32),
            pltpu.VMEM((NFOC * INNER.rows, W), F32),
            pltpu.VMEM((INNER.rows, W), F32),
        ],
        compiler_params=params(14),
        cost_estimate=pl.CostEstimate(flops=4_000_000_000, bytes_accessed=8_000_000, transcendentals=0),
    )(
        dose_rows,
        edge,
        spectra,
        target,
        hats,
        entry,
        inverse,
        interp,
        low(forward_table().T),
        low(inverse_table().T),
        low(interpolation_table().T),
        low(row_tables()[0]),
    )
    place_grad, place_band = placing_tables(corners)
    blocks = lax.all_to_all(blocks, "corner", 0, 0, tiled=True)
    return pl.pallas_call(
        finish_kernel,
        name="finish",
        out_shape=(
            jax.ShapeDtypeStruct((ROWS, ROWS), F32),
            jax.ShapeDtypeStruct((ROWS, ROWS), F32),
        ),
        in_specs=whole(4),
        out_specs=tuple(whole(2)),
        compiler_params=params(4),
    )(blocks, slope, low(place_grad), low(place_band))


def solution(mesh):
    return jax.shard_map(
        per_device,
        mesh=mesh,
        in_specs=(P("tile", None), P("tile", None), P(), P()),
        out_specs=(P("tile", "corner"), P("tile", "corner")),
        check_vma=False,
    )
```

```python
import math

import jax
import jax.numpy as jnp
import numpy as np
from jax import lax
from jax.experimental import pallas as pl
from jax.experimental.pallas import tpu as pltpu
from jax.sharding import PartitionSpec as P

STEEPNESS = 4.0
THRESHOLD = 1.0
SHARPNESS = 12.0

BF = jnp.bfloat16
F32 = jnp.float32

W = 1024
NF = 192
LANES = 256
TAPS = 25
RIM = TAPS // 2
ROWS = 128
NK = 12
NFOC = 4
NDOSE = 4
TAP_ROWS = 112
GRID = 384
EDGE = 32
TEDGE = 16
GRAD_ROWS = 48
BAND_ROWS = 32


class Plan:
    def __init__(self, share, rows, order, turn):
        self.share = share
        self.rows = rows
        self.order = order
        self.turn = turn


OUTER = Plan(14, 16, 40, 1.91284375)
INNER = Plan(24, 24, 48, 1.62425)
PLANS = (OUTER, OUTER, INNER, INNER, INNER, INNER, OUTER, OUTER)
STARTS = tuple(sum(plan.share for plan in PLANS[:n]) - RIM for n in range(len(PLANS)))
WINDOW = (0, 1, 7, 2, 6, 3, 4, 5)


def low(table):
    return jnp.asarray(np.asarray(table, np.float32)).astype(BF)


def forward_table():
    phase = np.outer(np.arange(NF) - NF // 2, np.arange(W)) % W
    angle = 2.0 * math.pi * phase / W
    scale = 1.0 / math.sqrt(W)
    table = np.zeros((W, 2 * LANES))
    table[:, :NF] = scale * np.cos(angle).T
    table[:, LANES : LANES + NF] = -scale * np.sin(angle).T
    return table


def half_grid():
    return (np.arange(GRID // 2) + 0.5) / GRID


def inverse_table():
    angle = 2.0 * math.pi * np.outer(np.arange(NF) - NF // 2, half_grid())
    scale = 1.0 / math.sqrt(W)
    table = np.zeros((LANES, 2 * LANES))
    table[:NF, : GRID // 2] = scale * np.cos(angle)
    table[:NF, LANES : LANES + GRID // 2] = scale * np.sin(angle)
    return table


def interpolation_table():
    table = np.zeros((2 * LANES, W))
    for first, points in ((0, half_grid()), (LANES, -half_grid())):
        where = np.arange(W)[None, :] / W - points[:, None]
        part = np.ones(where.shape)
        for order in range(1, NF):
            part += 2.0 * np.cos(2.0 * math.pi * order * where)
        table[first : first + GRID // 2] = part / GRID
    return table


def row_angles(order, left, right):
    return 2.0 * math.pi * (np.outer(np.arange(left), np.arange(right)) % order) / order


def complex_table(plan, angle):
    return plan.turn * np.block([[np.cos(angle), -np.sin(angle)], [np.sin(angle), np.cos(angle)]])


def tap_table(plan):
    u = plan.order
    table = complex_table(plan, row_angles(u, u, TAPS)).reshape(2, u, 2, TAPS)
    full = np.zeros((NFOC, 2, u, 2, TAP_ROWS))
    for focus in range(NFOC):
        full[focus, :, :, :, focus : TAPS * NFOC : NFOC] = table
    return full.reshape(NFOC * 2 * u, 2 * TAP_ROWS)


def window_table(plan):
    return complex_table(plan, -row_angles(plan.order, plan.order, plan.order))


def back_table(plan):
    angle = row_angles(plan.order, plan.order, plan.order)
    return plan.turn * np.concatenate([np.cos(angle), np.sin(angle)], axis=1)


def mix_table(plan, count=2):
    u, rows = plan.order, plan.rows
    table = complex_table(plan, row_angles(u, rows, u)).reshape(2, rows, 2, u)
    full = np.zeros((2, count, rows, count, 2, u))
    for q in range(count):
        full[:, q, :, q] = table
    return full.reshape(2 * count * rows, count * 2 * u)


def unmix_table(plan, count=4):
    u, rows = plan.order, plan.rows
    table = complex_table(plan, -row_angles(u, u, rows)).reshape(2, u, 2, rows)
    full = np.zeros((count, 2, u, 2, count, rows))
    for q in range(count):
        full[q, :, :, :, q] = table
    return full.reshape(count * 2 * u, 2 * count * rows)


def entry_table():
    parts = [forward_table()]
    places = {}
    first = W
    for plan in (INNER, OUTER):
        taps = tap_table(plan)
        half, width = taps.shape[0] // 2, taps.shape[1]
        part = np.zeros((half, 2 * LANES))
        part[:, :width] = taps[:half]
        part[:, LANES : LANES + width] = taps[half:]
        parts.append(part)
        places[plan] = slice(first, first + half)
        first += half
    return np.concatenate(parts), places


def row_tables():
    places = {}
    parts = []
    first = 0
    for plan in (INNER, OUTER):
        places[plan] = []
        for table in (window_table(plan), mix_table(plan), unmix_table(plan), back_table(plan)):
            rows, width = table.shape
            places[plan].append((slice(first, first + rows), slice(0, width)))
            part = np.zeros((-(-rows // 16) * 16, LANES))
            part[:rows, :width] = table
            parts.append(part)
            first += part.shape[0]
    return np.concatenate(parts), places


def placing_tables(count):
    grad = np.zeros((ROWS, count, GRAD_ROWS))
    band = np.zeros((ROWS, count, BAND_ROWS))
    for source in range(count):
        share, start = PLANS[WINDOW[source]].share, STARTS[WINDOW[source]]
        for row in range(share + 2 * RIM):
            if 0 <= start - RIM + row < ROWS:
                grad[start - RIM + row, source, row] = 1.0
        for row in range(share):
            if 0 <= start + row < ROWS:
                band[start + row, source, row] = 1.0
    return grad.reshape(ROWS, -1), band.reshape(ROWS, -1)


def dot(left, right):
    return jnp.dot(left, right, preferred_element_type=F32)


def here(values):
    corner = lax.axis_index("corner")
    value = jnp.int32(values[WINDOW[0]])
    for n in range(1, len(WINDOW)):
        value = jnp.where(corner == n, values[WINDOW[n]], value)
    return value


def by_plan(work):
    outer = here([int(plan is OUTER) for plan in PLANS]) == 1
    pl.when(outer)(lambda: work(OUTER))
    pl.when(jnp.logical_not(outer))(lambda: work(INNER))


def stacked(value):
    return jnp.concatenate([value[:, :LANES], value[:, LANES:]], axis=0).astype(BF)


def picked(count, length, first):
    row = lax.broadcasted_iota(jnp.int32, (count, length), 0) + first
    row = jnp.where(row >= length, row - length, row)
    column = lax.broadcasted_iota(jnp.int32, (count, length), 1)
    return jnp.where(row == column, 1.0, 0.0).astype(BF)


def edge_kernel(mask_ref, target_ref, dose_ref, out_ref, dose_rows_ref, mask_rows, target_rows, doses, sems):
    down = here(range(len(WINDOW))) < len(WINDOW) // 2
    mask_from = pl.multiple_of(jnp.where(down, ROWS - EDGE, 0), EDGE)
    target_from = pl.multiple_of(jnp.where(down, ROWS - TEDGE, 0), TEDGE)
    copies = [
        pltpu.make_async_copy(mask_ref.at[pl.ds(mask_from, EDGE)], mask_rows, sems.at[0]),
        pltpu.make_async_copy(target_ref.at[pl.ds(target_from, TEDGE)], target_rows, sems.at[1]),
        pltpu.make_async_copy(dose_ref, doses, sems.at[2]),
    ]
    for copy in copies:
        copy.start()
    for copy in copies:
        copy.wait()
    out_ref[:EDGE] = jnp.tanh(mask_rows[...]).astype(BF)
    out_ref[EDGE:] = target_rows[...].astype(F32).astype(BF)
    for d in range(NDOSE):
        dose_rows_ref[d : d + 1] = jnp.full((1, ROWS), doses[d])


def prepare_kernel(kernels_ref, mask_ref, entry_ref, hat_ref, spectra_ref, slope_ref, taps_ref, share_ref, sem):
    column = pl.multiple_of(lax.axis_index("corner") * ROWS, ROWS)
    share = jnp.tanh(mask_ref[:, pl.ds(column, ROWS)])
    share_ref[...] = 1.0 - share * share
    copy = pltpu.make_async_copy(share_ref, slope_ref, sem)
    copy.start()
    taps_ref[:, :, NFOC * TAPS - 4 :] = jnp.zeros((2, 2, TAP_ROWS - NFOC * TAPS + 4, 2 * NF), F32)
    places = entry_table()[1]

    def transform(plan):
        u = plan.order
        lane = lax.broadcasted_iota(jnp.int32, (TAP_ROWS, LANES), 1)
        table = jnp.concatenate(
            [
                entry_ref[places[plan], : 2 * TAP_ROWS],
                entry_ref[places[plan], LANES : LANES + 2 * TAP_ROWS],
            ],
            axis=0,
        )
        for kernel in range(0, NK, 2):
            slot = kernel // 2 % 2
            parts = []
            for q in range(2):
                for tap in range(TAPS):
                    taps_ref[slot, q, tap * NFOC : (tap + 1) * NFOC] = kernels_ref[kernel + q, tap]
                taps = taps_ref[slot, q]
                re = jnp.where(lane < NF, taps[:, :LANES], 0.0)
                im = jnp.where(lane < NF, pltpu.roll(taps, NF, 1)[:, :LANES], 0.0)
                parts.append(jnp.concatenate([re, im], axis=0).astype(BF))
            hats = dot(table, jnp.concatenate(parts, axis=1))
            for q in range(2):
                hat = hats[:, q * LANES : (q + 1) * LANES].reshape(NFOC, 2 * u, LANES)
                hat_ref[(kernel + q) * NFOC : (kernel + q + 1) * NFOC, : 2 * u] = hat

    by_plan(transform)
    field = jnp.tanh(mask_ref[...])
    spectra_ref[...] = dot(field.astype(BF), entry_ref[:W]).astype(BF)
    copy.wait()


def image_kernel(
    dose_ref,
    edge_ref,
    spectra_ref,
    target_ref,
    hat_ref,
    entry_ref,
    inverse_ref,
    interp_ref,
    forward_t_ref,
    inverse_t_ref,
    interp_t_ref,
    rows_ref,
    out_ref,
    mixed_ref,
    field_ref,
    aerial_ref,
    grad_ref,
    band_ref,
):
    places = row_tables()[1]

    def work(plan):
        u, count = plan.order, plan.rows
        scale = 1.0 / (plan.turn * plan.turn * plan.turn * u)
        window_rows, mix_rows, unmix_rows, back_rows = places[plan]
        start = here(STARTS)
        rows = spectra_ref[...]
        wanted = target_ref[...].astype(F32).astype(BF)
        first, first_wanted = start - RIM, start
        if plan is OUTER:
            rows = jnp.concatenate([dot(edge_ref[:EDGE], entry_ref[:W]).astype(BF), rows], axis=0)
            wanted = jnp.concatenate([edge_ref[EDGE:], wanted], axis=0)
            first, first_wanted = first + EDGE, first_wanted + TEDGE
        pick = picked(u, rows.shape[0], first)
        mask_hat = dot(rows_ref[window_rows], stacked(dot(pick, rows))) * scale
        mask_re = mask_hat[:u]
        mask_im = mask_hat[u:]
        band_ref[:count] = dot(picked(count, wanted.shape[0], first_wanted), wanted)
        for group in range(NFOC * NK // 4):
            stacks = []
            for pair in range(2):
                stack = []
                for q in range(2):
                    kernel = group * 4 + pair * 2 + q
                    hat = hat_ref[(kernel % NK) * NFOC + kernel // NK, : 2 * u]
                    stack.append(mask_re * hat[:u] - mask_im * hat[u:])
                    stack.append(mask_re * hat[u:] + mask_im * hat[:u])
                stacks.append(jnp.concatenate(stack, axis=0).astype(BF))
            mixed = dot(rows_ref[mix_rows], jnp.concatenate(stacks, axis=1))
            half = 2 * count
            parts = [mixed[:half, :LANES], mixed[:half, LANES:], mixed[half:, :LANES], mixed[half:, LANES:]]
            mixed_ref[group * 8 * count : (group + 1) * 8 * count] = jnp.concatenate(parts, axis=0).astype(BF)
        per_focus = 2 * NK * count
        slots = [
            (group * 8 * count + q * count, group * 8 * count + (4 + q) * count)
            for group in range(NK // 4)
            for q in range(4)
        ]
        coarse = []
        for focus in range(NFOC):
            fields = dot(mixed_ref[focus * per_focus : (focus + 1) * per_focus], inverse_ref[...])
            field_ref[focus * per_focus : (focus + 1) * per_focus] = fields
            squares = jnp.zeros((count, 2 * LANES), F32)
            cross = jnp.zeros((count, LANES), F32)
            for at_re, at_im in slots:
                re = fields[at_re : at_re + count]
                im = fields[at_im : at_im + count]
                squares = squares + (re * re + im * im)
                cross = cross + (im[:, :LANES] * re[:, LANES:] - re[:, :LANES] * im[:, LANES:])
            squares = squares[:, :LANES] + squares[:, LANES:]
            cross = 2.0 * cross
            coarse.append(jnp.concatenate([squares + cross, squares - cross], axis=1))
        coarse = jnp.concatenate(coarse, axis=0)
        coarse_high = coarse.astype(BF)
        coarse_low = (coarse - coarse_high.astype(F32)).astype(BF)
        both = dot(jnp.concatenate([coarse_high, coarse_low], axis=0), interp_ref[...])
        aerial_ref[: NFOC * count] = both[: NFOC * count] + both[NFOC * count :]
        local = lax.broadcasted_iota(jnp.int32, (count, ROWS), 0)
        pixel = lax.axis_index("tile") * ROWS + start + local
        valid = (local < plan.share) & (pixel >= 0) & (pixel < ROWS * lax.axis_size("tile"))
        valid = jnp.where(valid, 1.0, 0.0)
        doses = [dose_ref[d : d + 1] for d in range(NDOSE)]
        for chunk in range(W // ROWS):
            cols = slice(chunk * ROWS, (chunk + 1) * ROWS)
            high = None
            low_sum = None
            kept = []
            for focus in range(NFOC):
                aerial = aerial_ref[focus * count : (focus + 1) * count, cols]
                for d in range(NDOSE):
                    swing = jnp.tanh((0.5 * STEEPNESS * doses[d]) * aerial - 0.5 * STEEPNESS * THRESHOLD)
                    power = (0.5 * SHARPNESS / math.log(2.0)) * swing + 0.5 * SHARPNESS / math.log(2.0)
                    up = jnp.exp2(power)
                    down = jnp.exp2(-power)
                    high = up if high is None else high + up
                    low_sum = down if low_sum is None else low_sum + down
                    kept.append((swing, up, down))
            pixels = band_ref[:count, cols]
            top = jnp.log(high) / SHARPNESS
            bottom = -jnp.log(low_sum) / SHARPNESS
            band_ref[:count, cols] = top - bottom
            high_weight = valid * (top - pixels) / high
            low_weight = valid * (bottom - pixels) / low_sum
            for focus in range(NFOC):
                total = None
                for d in range(NDOSE):
                    swing, up, down = kept[focus * NDOSE + d]
                    term = (high_weight * up + low_weight * down) * (1.0 - swing * swing)
                    term = term * (0.5 * STEEPNESS * doses[d])
                    total = term if total is None else total + term
                grad_ref[focus * count : (focus + 1) * count, cols] = total
        coarse_grad = dot(grad_ref[: NFOC * count].astype(BF), interp_t_ref[...])
        acc_re = jnp.zeros((u, LANES), F32)
        acc_im = jnp.zeros((u, LANES), F32)
        stacks = []
        for focus in range(NFOC):
            part = coarse_grad[focus * count : (focus + 1) * count]
            both = part[:, :LANES] + part[:, LANES:]
            apart = part[:, :LANES] - part[:, LANES:]
            both = jnp.concatenate([both, both], axis=1)
            apart = jnp.concatenate([-apart, apart], axis=1)
            base = focus * per_focus
            field_grad = {}
            for at_re, at_im in slots:
                re = field_ref[base + at_re : base + at_re + count]
                im = field_ref[base + at_im : base + at_im + count]
                re_turned = jnp.concatenate([re[:, LANES:], re[:, :LANES]], axis=1)
                im_turned = jnp.concatenate([im[:, LANES:], im[:, :LANES]], axis=1)
                field_grad[at_re] = both * re + apart * im_turned
                field_grad[at_im] = both * im - apart * re_turned
            field_grad = jnp.concatenate([field_grad[at] for at in sorted(field_grad)], axis=0)
            mixed_grad = dot(field_grad.astype(BF), inverse_t_ref[...]).astype(BF)
            grads = [mixed_grad[group * 8 * count : (group + 1) * 8 * count] for group in range(NK // 4)]
            stacks.append(jnp.concatenate(grads, axis=1))
        for focus in range(NFOC):
            grads = dot(rows_ref[unmix_rows], stacks[focus])
            for group in range(NK // 4):
                lanes = slice(group * LANES, (group + 1) * LANES)
                for q in range(4):
                    grad_re = grads[2 * q * u : (2 * q + 1) * u, lanes]
                    grad_im = grads[(2 * q + 1) * u : (2 * q + 2) * u, lanes]
                    hat = hat_ref[(group * 4 + q) * NFOC + focus, : 2 * u]
                    acc_re = acc_re + (grad_re * hat[:u] + grad_im * hat[u:])
                    acc_im = acc_im + (grad_im * hat[:u] - grad_re * hat[u:])
        acc_re = acc_re * scale
        acc_im = acc_im * scale
        acc = jnp.concatenate(
            [jnp.concatenate([acc_re, acc_im], axis=1), jnp.concatenate([-acc_im, acc_re], axis=1)], axis=0
        )
        spectra_grad = dot(rows_ref[back_rows], acc.astype(BF))
        if u < GRAD_ROWS:
            spectra_grad = jnp.concatenate([spectra_grad, jnp.zeros((GRAD_ROWS - u, 2 * LANES), F32)], axis=0)
        mask_grad = dot(spectra_grad.astype(BF), forward_t_ref[...]).astype(BF)
        empty = jnp.zeros((BAND_ROWS - count, ROWS), F32)
        for block in range(W // ROWS):
            cols = slice(block * ROWS, (block + 1) * ROWS)
            out_ref[block, :GRAD_ROWS] = mask_grad[:, cols]
            out_ref[block, GRAD_ROWS:] = jnp.concatenate([band_ref[:count, cols], empty], axis=0).astype(BF)

    by_plan(work)


def finish_kernel(blocks_ref, slope_ref, place_grad_ref, place_band_ref, band_ref, grad_ref):
    count = blocks_ref.shape[0]
    grads = blocks_ref[:, :GRAD_ROWS].reshape(count * GRAD_ROWS, ROWS)
    grad_ref[...] = dot(place_grad_ref[...], grads) * slope_ref[...]
    bands = blocks_ref[:, GRAD_ROWS:].reshape(count * BAND_ROWS, ROWS)
    band_ref[...] = dot(place_band_ref[...], bands)


def params(mib):
    return pltpu.CompilerParams(vmem_limit_bytes=mib << 20)


def whole(count):
    return [pl.BlockSpec(memory_space=pltpu.VMEM)] * count


def per_device(mask_logits, target, kernels, dose_levels):
    tiles = lax.axis_size("tile")
    corners = lax.axis_size("corner")
    edge, dose_rows = pl.pallas_call(
        edge_kernel,
        name="edge",
        out_shape=(
            jax.ShapeDtypeStruct((EDGE + TEDGE, W), BF),
            jax.ShapeDtypeStruct((NDOSE, ROWS), F32),
        ),
        in_specs=[pl.BlockSpec(memory_space=pl.ANY)] * 3,
        out_specs=tuple(whole(2)),
        scratch_shapes=[
            pltpu.VMEM((EDGE, W), F32),
            pltpu.VMEM((TEDGE, W), jnp.int32),
            pltpu.SMEM((NDOSE,), F32),
            pltpu.SemaphoreType.DMA((3,)),
        ],
        compiler_params=params(2),
        cost_estimate=pl.CostEstimate(flops=2_000_000_000, bytes_accessed=0, transcendentals=0),
    )(*[pltpu.with_memory_space_constraint(x, pltpu.HBM) for x in (mask_logits, target, dose_levels)])
    pairs = []
    for i in range(tiles - 1):
        for c in range(corners):
            begin = STARTS[WINDOW[c]] - RIM
            if begin < 0:
                pairs.append((i * corners + c, (i + 1) * corners + c))
            elif begin + PLANS[WINDOW[c]].share + 2 * RIM > ROWS:
                pairs.append(((i + 1) * corners + c, i * corners + c))
    edge = lax.ppermute(edge, ("tile", "corner"), pairs)
    entry = low(entry_table()[0])
    inverse = low(inverse_table())
    interp = low(interpolation_table())
    count = NFOC * NK
    hats, spectra, slope = pl.pallas_call(
        prepare_kernel,
        name="prepare",
        out_shape=(
            jax.ShapeDtypeStruct((count, 2 * INNER.order, LANES), F32),
            jax.ShapeDtypeStruct((ROWS, 2 * LANES), BF),
            jax.ShapeDtypeStruct((ROWS, ROWS), F32),
        ),
        in_specs=whole(3),
        out_specs=tuple(whole(2)) + (pl.BlockSpec(memory_space=pltpu.HBM),),
        scratch_shapes=[
            pltpu.VMEM((2, 2, TAP_ROWS, 2 * NF), F32),
            pltpu.VMEM((ROWS, ROWS), F32),
            pltpu.SemaphoreType.DMA,
        ],
        compiler_params=params(6),
        cost_estimate=pl.CostEstimate(flops=1_200_000_000, bytes_accessed=0, transcendentals=0),
    )(kernels.transpose(1, 2, 0, 3), mask_logits, entry)
    blocks = pl.pallas_call(
        image_kernel,
        name="image",
        out_shape=jax.ShapeDtypeStruct((W // ROWS, GRAD_ROWS + BAND_ROWS, ROWS), BF),
        in_specs=whole(12),
        out_specs=pl.BlockSpec(memory_space=pltpu.VMEM),
        scratch_shapes=[
            pltpu.VMEM((2 * count * INNER.rows, LANES), BF),
            pltpu.VMEM((2 * count * INNER.rows, 2 * LANES), F32),
            pltpu.VMEM((NFOC * INNER.rows, W), F32),
            pltpu.VMEM((NFOC * INNER.rows, W), F32),
            pltpu.VMEM((INNER.rows, W), F32),
        ],
        compiler_params=params(14),
        cost_estimate=pl.CostEstimate(flops=4_000_000_000, bytes_accessed=8_000_000, transcendentals=0),
    )(
        dose_rows,
        edge,
        spectra,
        target,
        hats,
        entry,
        inverse,
        interp,
        low(forward_table().T),
        low(inverse_table().T),
        low(interpolation_table().T),
        low(row_tables()[0]),
    )
    place_grad, place_band = placing_tables(corners)
    blocks = lax.all_to_all(blocks, "corner", 0, 0, tiled=True)
    return pl.pallas_call(
        finish_kernel,
        name="finish",
        out_shape=(
            jax.ShapeDtypeStruct((ROWS, ROWS), F32),
            jax.ShapeDtypeStruct((ROWS, ROWS), F32),
        ),
        in_specs=whole(4),
        out_specs=tuple(whole(2)),
        compiler_params=params(4),
    )(blocks, slope, low(place_grad), low(place_band))


def solution(mesh):
    return jax.shard_map(
        per_device,
        mesh=mesh,
        in_specs=(P("tile", None), P("tile", None), P(), P()),
        out_specs=(P("tile", "corner"), P("tile", "corner")),
        check_vma=False,
    )
```

```python
import math

import jax
import jax.numpy as jnp
import numpy as np
from jax import lax
from jax.experimental import pallas as pl
from jax.experimental.pallas import tpu as pltpu
from jax.sharding import PartitionSpec as P

STEEPNESS = 4.0
THRESHOLD = 1.0
SHARPNESS = 12.0

BF = jnp.bfloat16
F32 = jnp.float32

W = 1024
NF = 192
LANES = 256
TAPS = 25
RIM = TAPS // 2
ROWS = 128
NK = 12
NFOC = 4
NDOSE = 4
TAP_ROWS = 112
GRID = 384
EDGE = 24
TEDGE = 16
SENT = 32
GRAD_ROWS = 48
BAND_ROWS = 32


class Plan:
    def __init__(self, share, rows, order, turn):
        self.share = share
        self.rows = rows
        self.order = order
        self.turn = turn


OUTER = Plan(14, 16, 40, 1.91284375)
INNER = Plan(24, 24, 48, 1.62425)
PLANS = (OUTER, OUTER, INNER, INNER, INNER, INNER, OUTER, OUTER)
STARTS = tuple(sum(plan.share for plan in PLANS[:n]) - RIM for n in range(len(PLANS)))
WINDOW = (0, 1, 7, 2, 6, 3, 4, 5)


def low(table):
    return jnp.asarray(np.asarray(table, np.float32)).astype(BF)


def forward_table():
    phase = np.outer(np.arange(NF) - NF // 2, np.arange(W)) % W
    angle = 2.0 * math.pi * phase / W
    scale = 1.0 / math.sqrt(W)
    table = np.zeros((W, 2 * LANES))
    table[:, :NF] = scale * np.cos(angle).T
    table[:, LANES : LANES + NF] = -scale * np.sin(angle).T
    return table


def half_grid():
    return (np.arange(GRID // 2) + 0.5) / GRID


def inverse_table():
    angle = 2.0 * math.pi * np.outer(np.arange(NF) - NF // 2, half_grid())
    scale = 1.0 / math.sqrt(W)
    table = np.zeros((LANES, 2 * LANES))
    table[:NF, : GRID // 2] = scale * np.cos(angle)
    table[:NF, LANES : LANES + GRID // 2] = scale * np.sin(angle)
    return table


def interpolation_table():
    table = np.zeros((2 * LANES, W))
    for first, points in ((0, half_grid()), (LANES, -half_grid())):
        where = np.arange(W)[None, :] / W - points[:, None]
        part = np.ones(where.shape)
        for order in range(1, NF):
            part += 2.0 * np.cos(2.0 * math.pi * order * where)
        table[first : first + GRID // 2] = part / GRID
    return table


def row_angles(order, left, right):
    return 2.0 * math.pi * (np.outer(np.arange(left), np.arange(right)) % order) / order


def complex_table(plan, angle):
    return plan.turn * np.block([[np.cos(angle), -np.sin(angle)], [np.sin(angle), np.cos(angle)]])


def tap_table(plan):
    u = plan.order
    table = complex_table(plan, row_angles(u, u, TAPS)).reshape(2, u, 2, TAPS)
    full = np.zeros((NFOC, 2, u, 2, TAP_ROWS))
    for focus in range(NFOC):
        full[focus, :, :, :, focus : TAPS * NFOC : NFOC] = table
    return full.reshape(NFOC * 2 * u, 2 * TAP_ROWS)


def window_table(plan):
    return complex_table(plan, -row_angles(plan.order, plan.order, plan.order))


def back_table(plan):
    angle = row_angles(plan.order, plan.order, plan.order)
    return plan.turn * np.concatenate([np.cos(angle), np.sin(angle)], axis=1)


def mix_table(plan, count=2):
    u, rows = plan.order, plan.rows
    table = complex_table(plan, row_angles(u, rows, u)).reshape(2, rows, 2, u)
    full = np.zeros((2, count, rows, count, 2, u))
    for q in range(count):
        full[:, q, :, q] = table
    return full.reshape(2 * count * rows, count * 2 * u)


def unmix_table(plan, count=4):
    u, rows = plan.order, plan.rows
    table = complex_table(plan, -row_angles(u, u, rows)).reshape(2, u, 2, rows)
    full = np.zeros((count, 2, u, 2, count, rows))
    for q in range(count):
        full[q, :, :, :, q] = table
    return full.reshape(count * 2 * u, 2 * count * rows)


def entry_table():
    parts = [forward_table()]
    places = {}
    first = W
    for plan in (INNER, OUTER):
        taps = tap_table(plan)
        half, width = taps.shape[0] // 2, taps.shape[1]
        part = np.zeros((half, 2 * LANES))
        part[:, :width] = taps[:half]
        part[:, LANES : LANES + width] = taps[half:]
        parts.append(part)
        places[plan] = slice(first, first + half)
        first += half
    return np.concatenate(parts), places


def row_tables():
    places = {}
    parts = []
    first = 0
    for plan in (INNER, OUTER):
        places[plan] = []
        for table in (window_table(plan), mix_table(plan), unmix_table(plan), back_table(plan)):
            rows, width = table.shape
            places[plan].append((slice(first, first + rows), slice(0, width)))
            part = np.zeros((-(-rows // 16) * 16, LANES))
            part[:rows, :width] = table
            parts.append(part)
            first += part.shape[0]
    return np.concatenate(parts), places


def placing_tables(count):
    grad = np.zeros((ROWS, count, GRAD_ROWS))
    band = np.zeros((ROWS, count, BAND_ROWS))
    for source in range(count):
        share, start = PLANS[WINDOW[source]].share, STARTS[WINDOW[source]]
        for row in range(share + 2 * RIM):
            if 0 <= start - RIM + row < ROWS:
                grad[start - RIM + row, source, row] = 1.0
        for row in range(share):
            if 0 <= start + row < ROWS:
                band[start + row, source, row] = 1.0
    return grad.reshape(ROWS, -1), band.reshape(ROWS, -1)


def dot(left, right):
    return jnp.dot(left, right, preferred_element_type=F32)


def here(values):
    corner = lax.axis_index("corner")
    value = jnp.int32(values[WINDOW[0]])
    for n in range(1, len(WINDOW)):
        value = jnp.where(corner == n, values[WINDOW[n]], value)
    return value


def by_plan(work):
    outer = here([int(plan is OUTER) for plan in PLANS]) == 1
    pl.when(outer)(lambda: work(OUTER))
    pl.when(jnp.logical_not(outer))(lambda: work(INNER))


def stacked(value):
    return jnp.concatenate([value[:, :LANES], value[:, LANES:]], axis=0).astype(BF)


def picked(count, length, first, sent, held):
    row = lax.broadcasted_iota(jnp.int32, (count, length), 0) + first
    row = jnp.where(row < 0, row + sent, jnp.where(row >= ROWS, row - ROWS, row + held))
    column = lax.broadcasted_iota(jnp.int32, (count, length), 1)
    return jnp.where(row == column, 1.0, 0.0).astype(BF)


def edge_kernel(mask_ref, target_ref, dose_ref, out_ref, dose_rows_ref, mask_rows, target_rows, doses, sems):
    down = here(range(len(WINDOW))) < len(WINDOW) // 2
    mask_from = pl.multiple_of(jnp.where(down, ROWS - EDGE, 0), 8)
    target_from = pl.multiple_of(jnp.where(down, ROWS - TEDGE, 0), TEDGE)
    copies = [
        pltpu.make_async_copy(mask_ref.at[pl.ds(mask_from, EDGE)], mask_rows, sems.at[0]),
        pltpu.make_async_copy(target_ref.at[pl.ds(target_from, TEDGE)], target_rows, sems.at[1]),
        pltpu.make_async_copy(dose_ref, doses, sems.at[2]),
    ]
    for copy in copies:
        copy.start()
    for copy in copies:
        copy.wait()
    wanted = target_rows[...].astype(F32)
    under = SENT - EDGE
    beside = [wanted[under:, first : first + LANES] for first in range(0, W, LANES)]
    rows = jnp.concatenate([jnp.tanh(mask_rows[...]), wanted[:under]], axis=0)
    out_ref[...] = jnp.concatenate([rows, jnp.concatenate(beside, axis=0)], axis=1).astype(BF)
    for d in range(NDOSE):
        dose_rows_ref[d : d + 1] = jnp.full((1, ROWS), doses[d])


def prepare_kernel(kernels_ref, mask_ref, entry_ref, hat_ref, spectra_ref, slope_ref, taps_ref, share_ref, sem):
    column = pl.multiple_of(lax.axis_index("corner") * ROWS, ROWS)
    share = jnp.tanh(mask_ref[:, pl.ds(column, ROWS)])
    share_ref[...] = 1.0 - share * share
    copy = pltpu.make_async_copy(share_ref, slope_ref, sem)
    copy.start()
    taps_ref[:, :, NFOC * TAPS - 4 :] = jnp.zeros((2, 2, TAP_ROWS - NFOC * TAPS + 4, 2 * NF), F32)
    places = entry_table()[1]

    def transform(plan):
        u = plan.order
        lane = lax.broadcasted_iota(jnp.int32, (TAP_ROWS, LANES), 1)
        table = jnp.concatenate(
            [
                entry_ref[places[plan], : 2 * TAP_ROWS],
                entry_ref[places[plan], LANES : LANES + 2 * TAP_ROWS],
            ],
            axis=0,
        )
        for kernel in range(0, NK, 2):
            slot = kernel // 2 % 2
            parts = []
            for q in range(2):
                for tap in range(TAPS):
                    taps_ref[slot, q, tap * NFOC : (tap + 1) * NFOC] = kernels_ref[kernel + q, tap]
                taps = taps_ref[slot, q]
                re = jnp.where(lane < NF, taps[:, :LANES], 0.0)
                im = jnp.where(lane < NF, pltpu.roll(taps, NF, 1)[:, :LANES], 0.0)
                parts.append(jnp.concatenate([re, im], axis=0).astype(BF))
            hats = dot(table, jnp.concatenate(parts, axis=1))
            for q in range(2):
                hat = hats[:, q * LANES : (q + 1) * LANES].reshape(NFOC, 2 * u, LANES)
                hat_ref[(kernel + q) * NFOC : (kernel + q + 1) * NFOC, : 2 * u] = hat

    by_plan(transform)
    field = jnp.tanh(mask_ref[...])
    spectra_ref[...] = dot(field.astype(BF), entry_ref[:W]).astype(BF)
    copy.wait()


def image_kernel(
    dose_ref,
    edge_ref,
    spectra_ref,
    target_ref,
    hat_ref,
    entry_ref,
    inverse_ref,
    interp_ref,
    forward_t_ref,
    inverse_t_ref,
    interp_t_ref,
    rows_ref,
    out_ref,
    mixed_ref,
    field_ref,
    aerial_ref,
    grad_ref,
    band_ref,
):
    places = row_tables()[1]

    def work(plan):
        u, count = plan.order, plan.rows
        scale = 1.0 / (plan.turn * plan.turn * plan.turn * u)
        window_rows, mix_rows, unmix_rows, back_rows = places[plan]
        start = here(STARTS)
        rows = spectra_ref[...]
        wanted = target_ref[...].astype(F32).astype(BF)
        edges = (0, 0, 0, 0)
        if plan is OUTER:
            rows = jnp.concatenate([dot(edge_ref[:, :W], entry_ref[:W]).astype(BF), rows], axis=0)
            under = SENT - EDGE
            beside = edge_ref[:, W:].astype(F32)
            beside = [beside[first : first + under] for first in range(0, SENT, under)]
            sent = [edge_ref[:, :W].astype(F32)[EDGE:], jnp.concatenate(beside, axis=1)]
            wanted = jnp.concatenate([jnp.concatenate(sent, axis=0).astype(BF), wanted], axis=0)
            edges = (EDGE, SENT, TEDGE, TEDGE)
        pick = picked(u, rows.shape[0], start - RIM, *edges[:2])
        mask_hat = dot(rows_ref[window_rows], stacked(dot(pick, rows))) * scale
        mask_re = mask_hat[:u]
        mask_im = mask_hat[u:]
        band_ref[:count] = dot(picked(count, wanted.shape[0], start, *edges[2:]), wanted)
        for group in range(NFOC * NK // 4):
            stacks = []
            for pair in range(2):
                stack = []
                for q in range(2):
                    kernel = group * 4 + pair * 2 + q
                    hat = hat_ref[(kernel % NK) * NFOC + kernel // NK, : 2 * u]
                    stack.append(mask_re * hat[:u] - mask_im * hat[u:])
                    stack.append(mask_re * hat[u:] + mask_im * hat[:u])
                stacks.append(jnp.concatenate(stack, axis=0).astype(BF))
            mixed = dot(rows_ref[mix_rows], jnp.concatenate(stacks, axis=1))
            half = 2 * count
            parts = [mixed[:half, :LANES], mixed[:half, LANES:], mixed[half:, :LANES], mixed[half:, LANES:]]
            mixed_ref[group * 8 * count : (group + 1) * 8 * count] = jnp.concatenate(parts, axis=0).astype(BF)
        per_focus = 2 * NK * count
        slots = [
            (group * 8 * count + q * count, group * 8 * count + (4 + q) * count)
            for group in range(NK // 4)
            for q in range(4)
        ]
        coarse = []
        for focus in range(NFOC):
            fields = dot(mixed_ref[focus * per_focus : (focus + 1) * per_focus], inverse_ref[...])
            field_ref[focus * per_focus : (focus + 1) * per_focus] = fields
            squares = jnp.zeros((count, 2 * LANES), F32)
            cross = jnp.zeros((count, LANES), F32)
            for at_re, at_im in slots:
                re = fields[at_re : at_re + count]
                im = fields[at_im : at_im + count]
                squares = squares + (re * re + im * im)
                cross = cross + (im[:, :LANES] * re[:, LANES:] - re[:, :LANES] * im[:, LANES:])
            squares = squares[:, :LANES] + squares[:, LANES:]
            cross = 2.0 * cross
            coarse.append(jnp.concatenate([squares + cross, squares - cross], axis=1))
        coarse = jnp.concatenate(coarse, axis=0)
        coarse_high = coarse.astype(BF)
        coarse_low = (coarse - coarse_high.astype(F32)).astype(BF)
        both = dot(jnp.concatenate([coarse_high, coarse_low], axis=0), interp_ref[...])
        aerial_ref[: NFOC * count] = both[: NFOC * count] + both[NFOC * count :]
        local = lax.broadcasted_iota(jnp.int32, (count, ROWS), 0)
        pixel = lax.axis_index("tile") * ROWS + start + local
        valid = (local < plan.share) & (pixel >= 0) & (pixel < ROWS * lax.axis_size("tile"))
        valid = jnp.where(valid, 1.0, 0.0)
        doses = [dose_ref[d : d + 1] for d in range(NDOSE)]
        for chunk in range(W // ROWS):
            cols = slice(chunk * ROWS, (chunk + 1) * ROWS)
            high = None
            low_sum = None
            kept = []
            for focus in range(NFOC):
                aerial = aerial_ref[focus * count : (focus + 1) * count, cols]
                for d in range(NDOSE):
                    swing = jnp.tanh((0.5 * STEEPNESS * doses[d]) * aerial - 0.5 * STEEPNESS * THRESHOLD)
                    power = (0.5 * SHARPNESS / math.log(2.0)) * swing + 0.5 * SHARPNESS / math.log(2.0)
                    up = jnp.exp2(power)
                    down = jnp.exp2(-power)
                    high = up if high is None else high + up
                    low_sum = down if low_sum is None else low_sum + down
                    kept.append((swing, up, down))
            pixels = band_ref[:count, cols]
            top = jnp.log(high) / SHARPNESS
            bottom = -jnp.log(low_sum) / SHARPNESS
            band_ref[:count, cols] = top - bottom
            high_weight = valid * (top - pixels) / high
            low_weight = valid * (bottom - pixels) / low_sum
            for focus in range(NFOC):
                total = None
                for d in range(NDOSE):
                    swing, up, down = kept[focus * NDOSE + d]
                    term = (high_weight * up + low_weight * down) * (1.0 - swing * swing)
                    term = term * (0.5 * STEEPNESS * doses[d])
                    total = term if total is None else total + term
                grad_ref[focus * count : (focus + 1) * count, cols] = total
        coarse_grad = dot(grad_ref[: NFOC * count].astype(BF), interp_t_ref[...])
        acc_re = jnp.zeros((u, LANES), F32)
        acc_im = jnp.zeros((u, LANES), F32)
        stacks = []
        for focus in range(NFOC):
            part = coarse_grad[focus * count : (focus + 1) * count]
            both = part[:, :LANES] + part[:, LANES:]
            apart = part[:, :LANES] - part[:, LANES:]
            both = jnp.concatenate([both, both], axis=1)
            apart = jnp.concatenate([-apart, apart], axis=1)
            base = focus * per_focus
            field_grad = {}
            for at_re, at_im in slots:
                re = field_ref[base + at_re : base + at_re + count]
                im = field_ref[base + at_im : base + at_im + count]
                re_turned = jnp.concatenate([re[:, LANES:], re[:, :LANES]], axis=1)
                im_turned = jnp.concatenate([im[:, LANES:], im[:, :LANES]], axis=1)
                field_grad[at_re] = both * re + apart * im_turned
                field_grad[at_im] = both * im - apart * re_turned
            field_grad = jnp.concatenate([field_grad[at] for at in sorted(field_grad)], axis=0)
            mixed_grad = dot(field_grad.astype(BF), inverse_t_ref[...]).astype(BF)
            grads = [mixed_grad[group * 8 * count : (group + 1) * 8 * count] for group in range(NK // 4)]
            stacks.append(jnp.concatenate(grads, axis=1))
        for focus in range(NFOC):
            grads = dot(rows_ref[unmix_rows], stacks[focus])
            for group in range(NK // 4):
                lanes = slice(group * LANES, (group + 1) * LANES)
                for q in range(4):
                    grad_re = grads[2 * q * u : (2 * q + 1) * u, lanes]
                    grad_im = grads[(2 * q + 1) * u : (2 * q + 2) * u, lanes]
                    hat = hat_ref[(group * 4 + q) * NFOC + focus, : 2 * u]
                    acc_re = acc_re + (grad_re * hat[:u] + grad_im * hat[u:])
                    acc_im = acc_im + (grad_im * hat[:u] - grad_re * hat[u:])
        acc_re = acc_re * scale
        acc_im = acc_im * scale
        acc = jnp.concatenate(
            [jnp.concatenate([acc_re, acc_im], axis=1), jnp.concatenate([-acc_im, acc_re], axis=1)], axis=0
        )
        spectra_grad = dot(rows_ref[back_rows], acc.astype(BF))
        if u < GRAD_ROWS:
            spectra_grad = jnp.concatenate([spectra_grad, jnp.zeros((GRAD_ROWS - u, 2 * LANES), F32)], axis=0)
        mask_grad = dot(spectra_grad.astype(BF), forward_t_ref[...]).astype(BF)
        empty = jnp.zeros((BAND_ROWS - count, ROWS), F32)
        for block in range(W // ROWS):
            cols = slice(block * ROWS, (block + 1) * ROWS)
            out_ref[block, :GRAD_ROWS] = mask_grad[:, cols]
            out_ref[block, GRAD_ROWS:] = jnp.concatenate([band_ref[:count, cols], empty], axis=0).astype(BF)

    by_plan(work)


def finish_kernel(blocks_ref, slope_ref, place_grad_ref, place_band_ref, band_ref, grad_ref):
    count = blocks_ref.shape[0]
    grads = blocks_ref[:, :GRAD_ROWS].reshape(count * GRAD_ROWS, ROWS)
    grad_ref[...] = dot(place_grad_ref[...], grads) * slope_ref[...]
    bands = blocks_ref[:, GRAD_ROWS:].reshape(count * BAND_ROWS, ROWS)
    band_ref[...] = dot(place_band_ref[...], bands)


def params(mib):
    return pltpu.CompilerParams(vmem_limit_bytes=mib << 20)


def whole(count):
    return [pl.BlockSpec(memory_space=pltpu.VMEM)] * count


def per_device(mask_logits, target, kernels, dose_levels):
    tiles = lax.axis_size("tile")
    corners = lax.axis_size("corner")
    edge, dose_rows = pl.pallas_call(
        edge_kernel,
        name="edge",
        out_shape=(
            jax.ShapeDtypeStruct((SENT, W + LANES), BF),
            jax.ShapeDtypeStruct((NDOSE, ROWS), F32),
        ),
        in_specs=[pl.BlockSpec(memory_space=pl.ANY)] * 3,
        out_specs=tuple(whole(2)),
        scratch_shapes=[
            pltpu.VMEM((EDGE, W), F32),
            pltpu.VMEM((TEDGE, W), jnp.int32),
            pltpu.SMEM((NDOSE,), F32),
            pltpu.SemaphoreType.DMA((3,)),
        ],
        compiler_params=params(2),
        cost_estimate=pl.CostEstimate(flops=2_000_000_000, bytes_accessed=0, transcendentals=0),
    )(*[pltpu.with_memory_space_constraint(x, pltpu.HBM) for x in (mask_logits, target, dose_levels)])
    pairs = []
    for i in range(tiles - 1):
        for c in range(corners):
            begin = STARTS[WINDOW[c]] - RIM
            if begin < 0:
                pairs.append((i * corners + c, (i + 1) * corners + c))
            elif begin + PLANS[WINDOW[c]].share + 2 * RIM > ROWS:
                pairs.append(((i + 1) * corners + c, i * corners + c))
    edge = lax.ppermute(edge, ("tile", "corner"), pairs)
    entry = low(entry_table()[0])
    inverse = low(inverse_table())
    interp = low(interpolation_table())
    count = NFOC * NK
    hats, spectra, slope = pl.pallas_call(
        prepare_kernel,
        name="prepare",
        out_shape=(
            jax.ShapeDtypeStruct((count, 2 * INNER.order, LANES), F32),
            jax.ShapeDtypeStruct((ROWS, 2 * LANES), BF),
            jax.ShapeDtypeStruct((ROWS, ROWS), F32),
        ),
        in_specs=whole(3),
        out_specs=tuple(whole(2)) + (pl.BlockSpec(memory_space=pltpu.HBM),),
        scratch_shapes=[
            pltpu.VMEM((2, 2, TAP_ROWS, 2 * NF), F32),
            pltpu.VMEM((ROWS, ROWS), F32),
            pltpu.SemaphoreType.DMA,
        ],
        compiler_params=params(6),
        cost_estimate=pl.CostEstimate(flops=1_200_000_000, bytes_accessed=0, transcendentals=0),
    )(kernels.transpose(1, 2, 0, 3), mask_logits, entry)
    blocks = pl.pallas_call(
        image_kernel,
        name="image",
        out_shape=jax.ShapeDtypeStruct((W // ROWS, GRAD_ROWS + BAND_ROWS, ROWS), BF),
        in_specs=whole(12),
        out_specs=pl.BlockSpec(memory_space=pltpu.VMEM),
        scratch_shapes=[
            pltpu.VMEM((2 * count * INNER.rows, LANES), BF),
            pltpu.VMEM((2 * count * INNER.rows, 2 * LANES), F32),
            pltpu.VMEM((NFOC * INNER.rows, W), F32),
            pltpu.VMEM((NFOC * INNER.rows, W), F32),
            pltpu.VMEM((INNER.rows, W), F32),
        ],
        compiler_params=params(14),
        cost_estimate=pl.CostEstimate(flops=4_000_000_000, bytes_accessed=8_000_000, transcendentals=0),
    )(
        dose_rows,
        edge,
        spectra,
        target,
        hats,
        entry,
        inverse,
        interp,
        low(forward_table().T),
        low(inverse_table().T),
        low(interpolation_table().T),
        low(row_tables()[0]),
    )
    place_grad, place_band = placing_tables(corners)
    blocks = lax.all_to_all(blocks, "corner", 0, 0, tiled=True)
    return pl.pallas_call(
        finish_kernel,
        name="finish",
        out_shape=(
            jax.ShapeDtypeStruct((ROWS, ROWS), F32),
            jax.ShapeDtypeStruct((ROWS, ROWS), F32),
        ),
        in_specs=whole(4),
        out_specs=tuple(whole(2)),
        compiler_params=params(4),
    )(blocks, slope, low(place_grad), low(place_band))


def solution(mesh):
    return jax.shard_map(
        per_device,
        mesh=mesh,
        in_specs=(P("tile", None), P("tile", None), P(), P()),
        out_specs=(P("tile", "corner"), P("tile", "corner")),
        check_vma=False,
    )
```

```python
import math

import jax
import jax.numpy as jnp
import numpy as np
from jax import lax
from jax.experimental import pallas as pl
from jax.experimental.pallas import tpu as pltpu
from jax.sharding import PartitionSpec as P

STEEPNESS = 4.0
THRESHOLD = 1.0
SHARPNESS = 12.0

BF = jnp.bfloat16
F32 = jnp.float32

W = 1024
NF = 192
LANES = 256
TAPS = 25
RIM = TAPS // 2
ROWS = 128
NK = 12
NFOC = 4
NDOSE = 4
TAP_ROWS = 112
GRID = 384
EDGE = 24
TEDGE = 16
SENT = 32
GRAD_ROWS = 48
BAND_ROWS = 32


class Plan:
    def __init__(self, share, rows, order, turn):
        self.share = share
        self.rows = rows
        self.order = order
        self.turn = turn


OUTER = Plan(14, 16, 40, 1.91284375)
INNER = Plan(24, 24, 48, 1.62425)
PLANS = (OUTER, OUTER, INNER, INNER, INNER, INNER, OUTER, OUTER)
STARTS = tuple(sum(plan.share for plan in PLANS[:n]) - RIM for n in range(len(PLANS)))
WINDOW = (0, 6, 7, 2, 1, 3, 4, 5)


def low(table):
    return jnp.asarray(np.asarray(table, np.float32)).astype(BF)


def forward_table():
    phase = np.outer(np.arange(NF) - NF // 2, np.arange(W)) % W
    angle = 2.0 * math.pi * phase / W
    scale = 1.0 / math.sqrt(W)
    table = np.zeros((W, 2 * LANES))
    table[:, :NF] = scale * np.cos(angle).T
    table[:, LANES : LANES + NF] = -scale * np.sin(angle).T
    return table


def half_grid():
    return (np.arange(GRID // 2) + 0.5) / GRID


def inverse_table():
    angle = 2.0 * math.pi * np.outer(np.arange(NF) - NF // 2, half_grid())
    scale = 1.0 / math.sqrt(W)
    table = np.zeros((LANES, 2 * LANES))
    table[:NF, : GRID // 2] = scale * np.cos(angle)
    table[:NF, LANES : LANES + GRID // 2] = scale * np.sin(angle)
    return table


def interpolation_table():
    table = np.zeros((2 * LANES, W))
    for first, points in ((0, half_grid()), (LANES, -half_grid())):
        where = np.arange(W)[None, :] / W - points[:, None]
        part = np.ones(where.shape)
        for order in range(1, NF):
            part += 2.0 * np.cos(2.0 * math.pi * order * where)
        table[first : first + GRID // 2] = part / GRID
    return table


def row_angles(order, left, right):
    return 2.0 * math.pi * (np.outer(np.arange(left), np.arange(right)) % order) / order


def complex_table(plan, angle):
    return plan.turn * np.block([[np.cos(angle), -np.sin(angle)], [np.sin(angle), np.cos(angle)]])


def tap_table(plan):
    u = plan.order
    table = complex_table(plan, row_angles(u, u, TAPS)).reshape(2, u, 2, TAPS)
    full = np.zeros((NFOC, 2, u, 2, TAP_ROWS))
    for focus in range(NFOC):
        full[focus, :, :, :, focus : TAPS * NFOC : NFOC] = table
    return full.reshape(NFOC * 2 * u, 2 * TAP_ROWS)


def window_table(plan):
    return complex_table(plan, -row_angles(plan.order, plan.order, plan.order))


def back_table(plan):
    angle = row_angles(plan.order, plan.order, plan.order)
    return plan.turn * np.concatenate([np.cos(angle), np.sin(angle)], axis=1)


def mix_table(plan, count=2):
    u, rows = plan.order, plan.rows
    table = complex_table(plan, row_angles(u, rows, u)).reshape(2, rows, 2, u)
    full = np.zeros((2, count, rows, count, 2, u))
    for q in range(count):
        full[:, q, :, q] = table
    return full.reshape(2 * count * rows, count * 2 * u)


def unmix_table(plan, count=4):
    u, rows = plan.order, plan.rows
    table = complex_table(plan, -row_angles(u, u, rows)).reshape(2, u, 2, rows)
    full = np.zeros((count, 2, u, 2, count, rows))
    for q in range(count):
        full[q, :, :, :, q] = table
    return full.reshape(count * 2 * u, 2 * count * rows)


def entry_table():
    parts = [forward_table()]
    places = {}
    first = W
    for plan in (INNER, OUTER):
        taps = tap_table(plan)
        half, width = taps.shape[0] // 2, taps.shape[1]
        part = np.zeros((half, 2 * LANES))
        part[:, :width] = taps[:half]
        part[:, LANES : LANES + width] = taps[half:]
        parts.append(part)
        places[plan] = slice(first, first + half)
        first += half
    return np.concatenate(parts), places


def row_tables():
    places = {}
    parts = []
    first = 0
    for plan in (INNER, OUTER):
        places[plan] = []
        for table in (window_table(plan), mix_table(plan), unmix_table(plan), back_table(plan)):
            rows, width = table.shape
            places[plan].append((slice(first, first + rows), slice(0, width)))
            part = np.zeros((-(-rows // 16) * 16, LANES))
            part[:rows, :width] = table
            parts.append(part)
            first += part.shape[0]
    return np.concatenate(parts), places


def placing_tables(count):
    grad = np.zeros((ROWS, count, GRAD_ROWS))
    band = np.zeros((ROWS, count, BAND_ROWS))
    for source in range(count):
        share, start = PLANS[WINDOW[source]].share, STARTS[WINDOW[source]]
        for row in range(share + 2 * RIM):
            if 0 <= start - RIM + row < ROWS:
                grad[start - RIM + row, source, row] = 1.0
        for row in range(share):
            if 0 <= start + row < ROWS:
                band[start + row, source, row] = 1.0
    return grad.reshape(ROWS, -1), band.reshape(ROWS, -1)


def dot(left, right):
    return jnp.dot(left, right, preferred_element_type=F32)


def here(values):
    corner = lax.axis_index("corner")
    value = jnp.int32(values[WINDOW[0]])
    for n in range(1, len(WINDOW)):
        value = jnp.where(corner == n, values[WINDOW[n]], value)
    return value


def by_plan(work):
    outer = here([int(plan is OUTER) for plan in PLANS]) == 1
    pl.when(outer)(lambda: work(OUTER))
    pl.when(jnp.logical_not(outer))(lambda: work(INNER))


def stacked(value):
    return jnp.concatenate([value[:, :LANES], value[:, LANES:]], axis=0).astype(BF)


def picked(count, length, first, sent, held):
    row = lax.broadcasted_iota(jnp.int32, (count, length), 0) + first
    row = jnp.where(row < 0, row + sent, jnp.where(row >= ROWS, row - ROWS, row + held))
    column = lax.broadcasted_iota(jnp.int32, (count, length), 1)
    return jnp.where(row == column, 1.0, 0.0).astype(BF)


def edge_kernel(mask_ref, target_ref, dose_ref, out_ref, dose_rows_ref, mask_rows, target_rows, doses, sems):
    down = here(range(len(WINDOW))) < len(WINDOW) // 2
    mask_from = pl.multiple_of(jnp.where(down, ROWS - EDGE, 0), 8)
    target_from = pl.multiple_of(jnp.where(down, ROWS - TEDGE, 0), TEDGE)
    copies = [
        pltpu.make_async_copy(mask_ref.at[pl.ds(mask_from, EDGE)], mask_rows, sems.at[0]),
        pltpu.make_async_copy(target_ref.at[pl.ds(target_from, TEDGE)], target_rows, sems.at[1]),
        pltpu.make_async_copy(dose_ref, doses, sems.at[2]),
    ]
    for copy in copies:
        copy.start()
    for copy in copies:
        copy.wait()
    wanted = target_rows[...].astype(F32)
    under = SENT - EDGE
    beside = [wanted[under:, first : first + LANES] for first in range(0, W, LANES)]
    rows = jnp.concatenate([jnp.tanh(mask_rows[...]), wanted[:under]], axis=0)
    out_ref[...] = jnp.concatenate([rows, jnp.concatenate(beside, axis=0)], axis=1).astype(BF)
    for d in range(NDOSE):
        dose_rows_ref[d : d + 1] = jnp.full((1, ROWS), doses[d])


def prepare_kernel(kernels_ref, mask_ref, entry_ref, hat_ref, spectra_ref, slope_ref, taps_ref, share_ref, sem):
    column = pl.multiple_of(lax.axis_index("corner") * ROWS, ROWS)
    share = jnp.tanh(mask_ref[:, pl.ds(column, ROWS)])
    share_ref[...] = 1.0 - share * share
    copy = pltpu.make_async_copy(share_ref, slope_ref, sem)
    copy.start()
    taps_ref[:, :, NFOC * TAPS - 4 :] = jnp.zeros((2, 2, TAP_ROWS - NFOC * TAPS + 4, 2 * NF), F32)
    places = entry_table()[1]

    def transform(plan):
        u = plan.order
        lane = lax.broadcasted_iota(jnp.int32, (TAP_ROWS, LANES), 1)
        table = jnp.concatenate(
            [
                entry_ref[places[plan], : 2 * TAP_ROWS],
                entry_ref[places[plan], LANES : LANES + 2 * TAP_ROWS],
            ],
            axis=0,
        )
        for kernel in range(0, NK, 2):
            slot = kernel // 2 % 2
            parts = []
            for q in range(2):
                for tap in range(TAPS):
                    taps_ref[slot, q, tap * NFOC : (tap + 1) * NFOC] = kernels_ref[kernel + q, tap]
                taps = taps_ref[slot, q]
                re = jnp.where(lane < NF, taps[:, :LANES], 0.0)
                im = jnp.where(lane < NF, pltpu.roll(taps, NF, 1)[:, :LANES], 0.0)
                parts.append(jnp.concatenate([re, im], axis=0).astype(BF))
            hats = dot(table, jnp.concatenate(parts, axis=1))
            for q in range(2):
                hat = hats[:, q * LANES : (q + 1) * LANES].reshape(NFOC, 2 * u, LANES)
                hat_ref[(kernel + q) * NFOC : (kernel + q + 1) * NFOC, : 2 * u] = hat

    by_plan(transform)
    field = jnp.tanh(mask_ref[...])
    spectra_ref[...] = dot(field.astype(BF), entry_ref[:W]).astype(BF)
    copy.wait()


def image_kernel(
    dose_ref,
    edge_ref,
    spectra_ref,
    target_ref,
    hat_ref,
    entry_ref,
    inverse_ref,
    interp_ref,
    forward_t_ref,
    inverse_t_ref,
    interp_t_ref,
    rows_ref,
    out_ref,
    mixed_ref,
    field_ref,
    aerial_ref,
    grad_ref,
    band_ref,
):
    places = row_tables()[1]

    def work(plan):
        u, count = plan.order, plan.rows
        scale = 1.0 / (plan.turn * plan.turn * plan.turn * u)
        window_rows, mix_rows, unmix_rows, back_rows = places[plan]
        start = here(STARTS)
        rows = spectra_ref[...]
        wanted = target_ref[...].astype(F32).astype(BF)
        edges = (0, 0, 0, 0)
        if plan is OUTER:
            rows = jnp.concatenate([dot(edge_ref[:, :W], entry_ref[:W]).astype(BF), rows], axis=0)
            under = SENT - EDGE
            beside = edge_ref[:, W:].astype(F32)
            beside = [beside[first : first + under] for first in range(0, SENT, under)]
            sent = [edge_ref[:, :W].astype(F32)[EDGE:], jnp.concatenate(beside, axis=1)]
            wanted = jnp.concatenate([jnp.concatenate(sent, axis=0).astype(BF), wanted], axis=0)
            edges = (EDGE, SENT, TEDGE, TEDGE)
        pick = picked(u, rows.shape[0], start - RIM, *edges[:2])
        mask_hat = dot(rows_ref[window_rows], stacked(dot(pick, rows))) * scale
        mask_re = mask_hat[:u]
        mask_im = mask_hat[u:]
        band_ref[:count] = dot(picked(count, wanted.shape[0], start, *edges[2:]), wanted)
        for group in range(NFOC * NK // 4):
            stacks = []
            for pair in range(2):
                stack = []
                for q in range(2):
                    kernel = group * 4 + pair * 2 + q
                    hat = hat_ref[(kernel % NK) * NFOC + kernel // NK, : 2 * u]
                    stack.append(mask_re * hat[:u] - mask_im * hat[u:])
                    stack.append(mask_re * hat[u:] + mask_im * hat[:u])
                stacks.append(jnp.concatenate(stack, axis=0).astype(BF))
            mixed = dot(rows_ref[mix_rows], jnp.concatenate(stacks, axis=1))
            half = 2 * count
            parts = [mixed[:half, :LANES], mixed[:half, LANES:], mixed[half:, :LANES], mixed[half:, LANES:]]
            mixed_ref[group * 8 * count : (group + 1) * 8 * count] = jnp.concatenate(parts, axis=0).astype(BF)
        per_focus = 2 * NK * count
        slots = [
            (group * 8 * count + q * count, group * 8 * count + (4 + q) * count)
            for group in range(NK // 4)
            for q in range(4)
        ]
        coarse = []
        for focus in range(NFOC):
            fields = dot(mixed_ref[focus * per_focus : (focus + 1) * per_focus], inverse_ref[...])
            field_ref[focus * per_focus : (focus + 1) * per_focus] = fields
            squares = jnp.zeros((count, 2 * LANES), F32)
            cross = jnp.zeros((count, LANES), F32)
            for at_re, at_im in slots:
                re = fields[at_re : at_re + count]
                im = fields[at_im : at_im + count]
                squares = squares + (re * re + im * im)
                cross = cross + (im[:, :LANES] * re[:, LANES:] - re[:, :LANES] * im[:, LANES:])
            squares = squares[:, :LANES] + squares[:, LANES:]
            cross = 2.0 * cross
            coarse.append(jnp.concatenate([squares + cross, squares - cross], axis=1))
        coarse = jnp.concatenate(coarse, axis=0)
        coarse_high = coarse.astype(BF)
        coarse_low = (coarse - coarse_high.astype(F32)).astype(BF)
        both = dot(jnp.concatenate([coarse_high, coarse_low], axis=0), interp_ref[...])
        aerial_ref[: NFOC * count] = both[: NFOC * count] + both[NFOC * count :]
        local = lax.broadcasted_iota(jnp.int32, (count, ROWS), 0)
        pixel = lax.axis_index("tile") * ROWS + start + local
        valid = (local < plan.share) & (pixel >= 0) & (pixel < ROWS * lax.axis_size("tile"))
        valid = jnp.where(valid, 1.0, 0.0)
        doses = [dose_ref[d : d + 1] for d in range(NDOSE)]
        for chunk in range(W // ROWS):
            cols = slice(chunk * ROWS, (chunk + 1) * ROWS)
            high = None
            low_sum = None
            kept = []
            for focus in range(NFOC):
                aerial = aerial_ref[focus * count : (focus + 1) * count, cols]
                for d in range(NDOSE):
                    swing = jnp.tanh((0.5 * STEEPNESS * doses[d]) * aerial - 0.5 * STEEPNESS * THRESHOLD)
                    power = (0.5 * SHARPNESS / math.log(2.0)) * swing + 0.5 * SHARPNESS / math.log(2.0)
                    up = jnp.exp2(power)
                    down = jnp.exp2(-power)
                    high = up if high is None else high + up
                    low_sum = down if low_sum is None else low_sum + down
                    kept.append((swing, up, down))
            pixels = band_ref[:count, cols]
            top = jnp.log(high) / SHARPNESS
            bottom = -jnp.log(low_sum) / SHARPNESS
            band_ref[:count, cols] = top - bottom
            high_weight = valid * (top - pixels) / high
            low_weight = valid * (bottom - pixels) / low_sum
            for focus in range(NFOC):
                total = None
                for d in range(NDOSE):
                    swing, up, down = kept[focus * NDOSE + d]
                    term = (high_weight * up + low_weight * down) * (1.0 - swing * swing)
                    term = term * (0.5 * STEEPNESS * doses[d])
                    total = term if total is None else total + term
                grad_ref[focus * count : (focus + 1) * count, cols] = total
        coarse_grad = dot(grad_ref[: NFOC * count].astype(BF), interp_t_ref[...])
        acc_re = jnp.zeros((u, LANES), F32)
        acc_im = jnp.zeros((u, LANES), F32)
        stacks = []
        for focus in range(NFOC):
            part = coarse_grad[focus * count : (focus + 1) * count]
            both = part[:, :LANES] + part[:, LANES:]
            apart = part[:, :LANES] - part[:, LANES:]
            both = jnp.concatenate([both, both], axis=1)
            apart = jnp.concatenate([-apart, apart], axis=1)
            base = focus * per_focus
            field_grad = {}
            for at_re, at_im in slots:
                re = field_ref[base + at_re : base + at_re + count]
                im = field_ref[base + at_im : base + at_im + count]
                re_turned = jnp.concatenate([re[:, LANES:], re[:, :LANES]], axis=1)
                im_turned = jnp.concatenate([im[:, LANES:], im[:, :LANES]], axis=1)
                field_grad[at_re] = both * re + apart * im_turned
                field_grad[at_im] = both * im - apart * re_turned
            field_grad = jnp.concatenate([field_grad[at] for at in sorted(field_grad)], axis=0)
            mixed_grad = dot(field_grad.astype(BF), inverse_t_ref[...]).astype(BF)
            grads = [mixed_grad[group * 8 * count : (group + 1) * 8 * count] for group in range(NK // 4)]
            stacks.append(jnp.concatenate(grads, axis=1))
        for focus in range(NFOC):
            grads = dot(rows_ref[unmix_rows], stacks[focus])
            for group in range(NK // 4):
                lanes = slice(group * LANES, (group + 1) * LANES)
                for q in range(4):
                    grad_re = grads[2 * q * u : (2 * q + 1) * u, lanes]
                    grad_im = grads[(2 * q + 1) * u : (2 * q + 2) * u, lanes]
                    hat = hat_ref[(group * 4 + q) * NFOC + focus, : 2 * u]
                    acc_re = acc_re + (grad_re * hat[:u] + grad_im * hat[u:])
                    acc_im = acc_im + (grad_im * hat[:u] - grad_re * hat[u:])
        acc_re = acc_re * scale
        acc_im = acc_im * scale
        acc = jnp.concatenate(
            [jnp.concatenate([acc_re, acc_im], axis=1), jnp.concatenate([-acc_im, acc_re], axis=1)], axis=0
        )
        spectra_grad = dot(rows_ref[back_rows], acc.astype(BF))
        if u < GRAD_ROWS:
            spectra_grad = jnp.concatenate([spectra_grad, jnp.zeros((GRAD_ROWS - u, 2 * LANES), F32)], axis=0)
        mask_grad = dot(spectra_grad.astype(BF), forward_t_ref[...]).astype(BF)
        empty = jnp.zeros((BAND_ROWS - count, ROWS), F32)
        for block in range(W // ROWS):
            cols = slice(block * ROWS, (block + 1) * ROWS)
            out_ref[block, :GRAD_ROWS] = mask_grad[:, cols]
            out_ref[block, GRAD_ROWS:] = jnp.concatenate([band_ref[:count, cols], empty], axis=0).astype(BF)

    by_plan(work)


def finish_kernel(blocks_ref, slope_ref, place_grad_ref, place_band_ref, band_ref, grad_ref):
    count = blocks_ref.shape[0]
    grads = blocks_ref[:, :GRAD_ROWS].reshape(count * GRAD_ROWS, ROWS)
    grad_ref[...] = dot(place_grad_ref[...], grads) * slope_ref[...]
    bands = blocks_ref[:, GRAD_ROWS:].reshape(count * BAND_ROWS, ROWS)
    band_ref[...] = dot(place_band_ref[...], bands)


def params(mib):
    return pltpu.CompilerParams(vmem_limit_bytes=mib << 20)


def whole(count):
    return [pl.BlockSpec(memory_space=pltpu.VMEM)] * count


def per_device(mask_logits, target, kernels, dose_levels):
    tiles = lax.axis_size("tile")
    corners = lax.axis_size("corner")
    edge, dose_rows = pl.pallas_call(
        edge_kernel,
        name="edge",
        out_shape=(
            jax.ShapeDtypeStruct((SENT, W + LANES), BF),
            jax.ShapeDtypeStruct((NDOSE, ROWS), F32),
        ),
        in_specs=[pl.BlockSpec(memory_space=pl.ANY)] * 3,
        out_specs=tuple(whole(2)),
        scratch_shapes=[
            pltpu.VMEM((EDGE, W), F32),
            pltpu.VMEM((TEDGE, W), jnp.int32),
            pltpu.SMEM((NDOSE,), F32),
            pltpu.SemaphoreType.DMA((3,)),
        ],
        compiler_params=params(2),
        cost_estimate=pl.CostEstimate(flops=2_000_000_000, bytes_accessed=0, transcendentals=0),
    )(*[pltpu.with_memory_space_constraint(x, pltpu.HBM) for x in (mask_logits, target, dose_levels)])
    pairs = []
    for i in range(tiles - 1):
        for c in range(corners):
            begin = STARTS[WINDOW[c]] - RIM
            if begin < 0:
                pairs.append((i * corners + c, (i + 1) * corners + c))
            elif begin + PLANS[WINDOW[c]].share + 2 * RIM > ROWS:
                pairs.append(((i + 1) * corners + c, i * corners + c))
    edge = lax.ppermute(edge, ("tile", "corner"), pairs)
    entry = low(entry_table()[0])
    inverse = low(inverse_table())
    interp = low(interpolation_table())
    count = NFOC * NK
    hats, spectra, slope = pl.pallas_call(
        prepare_kernel,
        name="prepare",
        out_shape=(
            jax.ShapeDtypeStruct((count, 2 * INNER.order, LANES), F32),
            jax.ShapeDtypeStruct((ROWS, 2 * LANES), BF),
            jax.ShapeDtypeStruct((ROWS, ROWS), F32),
        ),
        in_specs=whole(3),
        out_specs=tuple(whole(2)) + (pl.BlockSpec(memory_space=pltpu.HBM),),
        scratch_shapes=[
            pltpu.VMEM((2, 2, TAP_ROWS, 2 * NF), F32),
            pltpu.VMEM((ROWS, ROWS), F32),
            pltpu.SemaphoreType.DMA,
        ],
        compiler_params=params(6),
        cost_estimate=pl.CostEstimate(flops=1_200_000_000, bytes_accessed=0, transcendentals=0),
    )(kernels.transpose(1, 2, 0, 3), mask_logits, entry)
    blocks = pl.pallas_call(
        image_kernel,
        name="image",
        out_shape=jax.ShapeDtypeStruct((W // ROWS, GRAD_ROWS + BAND_ROWS, ROWS), BF),
        in_specs=whole(12),
        out_specs=pl.BlockSpec(memory_space=pltpu.VMEM),
        scratch_shapes=[
            pltpu.VMEM((2 * count * INNER.rows, LANES), BF),
            pltpu.VMEM((2 * count * INNER.rows, 2 * LANES), F32),
            pltpu.VMEM((NFOC * INNER.rows, W), F32),
            pltpu.VMEM((NFOC * INNER.rows, W), F32),
            pltpu.VMEM((INNER.rows, W), F32),
        ],
        compiler_params=params(14),
        cost_estimate=pl.CostEstimate(flops=4_000_000_000, bytes_accessed=8_000_000, transcendentals=0),
    )(
        dose_rows,
        edge,
        spectra,
        target,
        hats,
        entry,
        inverse,
        interp,
        low(forward_table().T),
        low(inverse_table().T),
        low(interpolation_table().T),
        low(row_tables()[0]),
    )
    place_grad, place_band = placing_tables(corners)
    blocks = lax.all_to_all(blocks, "corner", 0, 0, tiled=True)
    return pl.pallas_call(
        finish_kernel,
        name="finish",
        out_shape=(
            jax.ShapeDtypeStruct((ROWS, ROWS), F32),
            jax.ShapeDtypeStruct((ROWS, ROWS), F32),
        ),
        in_specs=whole(4),
        out_specs=tuple(whole(2)),
        compiler_params=params(4),
    )(blocks, slope, low(place_grad), low(place_band))


def solution(mesh):
    return jax.shard_map(
        per_device,
        mesh=mesh,
        in_specs=(P("tile", None), P("tile", None), P(), P()),
        out_specs=(P("tile", "corner"), P("tile", "corner")),
        check_vma=False,
    )
```
